128 devices in a mesh: expert: 32 (over y, x, z_lo), tensor: 4 (over z_hi, core).
Axes of the slice: x: 4, y: 4, z: 4 (z_hi: 2, z_lo: 2; z = z_hi * 2 + z_lo), core: 2. Of those that a mesh axis runs over, the one named last changes fastest.
Arguments:
- master: float32 [224, 128, 2048], P('expert', None, 'tensor'), may hold values from -0.0625 to 0.0625
- grad: bfloat16 [224, 128, 2048], P('expert', None, 'tensor'), may hold values from -6 to 6
- moment_one: float32 [224, 128, 2048], P('expert', None, 'tensor'), may hold values from -4 to 4
- moment_two: float32 [224, 128, 2048], P('expert', None, 'tensor'), may hold values from 0.05 to 4
- context: bfloat16 [512, 4096], P('expert', 'tensor'), may hold values from -6 to 6
- out_weight: bfloat16 [4096, 7168], P('tensor', 'expert'), may hold values from -0.09375 to 0.09375
- hidden: bfloat16 [512, 7168], P('expert'), may hold values from -6 to 6
- norm_gain: float32 [7168], replicated, may hold values from 0.25 to 1.75
- route: int32 [512], replicated, may hold values from 0 to 3
- plan: int32 [1024], replicated, may hold values from 0 to 223, as said below
Outputs:
- new_master: float32 [224, 128, 2048], P('expert', None, 'tensor')
- new_first: float32 [224, 128, 2048], P('expert', None, 'tensor')
- new_second: float32 [224, 128, 2048], P('expert', None, 'tensor')
- rollout: bfloat16 [1024, 128, 2048], P('expert', None, 'tensor')
- activation: bfloat16 [512, 2048], P('expert', 'tensor')
The draws below stay inside these ranges and needn't reach their ends.
Inputs may be any that keep to these rules, and one draw needn't show every extreme that they name: `plan`: entry o * 32 + j names the block in slot j of rollout owner o; block b lies on index b // 7 of expert in training; an owner takes at most 2 of its blocks from one training index.
All inputs are finite; a program needn't handle non-finite values.
Results may differ from the reference program's by a relative error of at most 0.0058.
Values may be sent and summed in bfloat16 or wider, within the bound.
A program may use at most 128 MiB of HBM per device.

```python
import math
import jax
import jax.numpy as jnp
from jax import lax

D = 7168
F = 2048
EXPERTS = 4
BR = 128
CAP = 2
SLOTS = 32
HV = 4096
BLK_E = 56
BLOCKS = 224
BLK_DEV = 7
TOK = 512
N_EXPERT = 32


def draw_plan(key, part):
    key = jax.random.fold_in(key, 11)
    key_hot, key_score, key_local, key_order = jax.random.split(key, 4)
    pairs = SLOTS // CAP
    hot_expert = jax.random.randint(key_hot, (), 0, EXPERTS)
    senders = jnp.arange(N_EXPERT, dtype=jnp.int32)
    first_expert = senders * BLK_DEV // BLK_E
    last_expert = ((senders + 1) * BLK_DEV - 1) // BLK_E
    holds_hot = ((first_expert == hot_expert) | (last_expert == hot_expert)).astype(jnp.int32)
    score = jax.random.randint(key_score, (N_EXPERT, N_EXPERT), 0, 1000) + 400 * holds_hot[None, :]
    score = score * N_EXPERT + senders[None, :]
    unused, chosen = lax.top_k(score, pairs)
    local = jax.random.randint(key_local, (N_EXPERT, pairs, CAP), 0, BLK_DEV)
    blocks = (chosen[:, :, None] * BLK_DEV + local).reshape(N_EXPERT, SLOTS)
    order_score = jax.random.randint(key_order, (N_EXPERT, SLOTS), 0, 4096) * SLOTS + jnp.arange(SLOTS, dtype=jnp.int32)[None, :]
    order = jnp.argsort(order_score, axis=1, stable=True)
    return jnp.take_along_axis(blocks, order, axis=1).reshape(N_EXPERT * SLOTS).astype(jnp.int32)


def with_ends(result, key, smallest, high):
    dims = result.shape
    spot = [jax.random.randint(jax.random.fold_in(key, axis), (), 0, dims[axis]) for axis in range(len(dims))]
    result = result.at[tuple(spot)].set(smallest)
    longest = dims.index(max(dims))
    spot[longest] = (spot[longest] + 1) % dims[longest]
    return result.at[tuple(spot)].set(high)


def block_levels(key, extent, pieces, least, top_value):
    def one(axis_at, parts):
        draws = jax.random.uniform(jax.random.fold_in(jax.random.fold_in(key, 6), axis_at), (parts,), jnp.float32, least / len(pieces), top_value / len(pieces))
        return jnp.repeat(jnp.exp(draws), extent[axis_at] // parts).reshape((-1,) + (1,) * (len(extent) - axis_at - 1))

    factor_of = one(*pieces[0])
    for cut in pieces[1:]:
        factor_of = factor_of * one(*cut)
    return factor_of


def gaussian(key, extent, width, most, shards=(), kind=jnp.bfloat16):
    result = width * jax.random.normal(key, extent, jnp.float32)
    if shards:
        result = result * block_levels(key, extent, shards, -0.22, 0.18)
    return jnp.clip(result, -most, most).astype(kind)


def setup_inputs(seed: int = 0) -> dict:
    key_of = jax.random.split(jax.random.key(seed), 11)
    return {
        "master": gaussian(key_of[0], (BLOCKS, BR, F), D ** -0.5, 0.0625, ((0, 32), (2, 4)), jnp.float32),
        "grad": gaussian(key_of[1], (BLOCKS, BR, F), 1.0, 6.0, ((0, 32), (2, 4))),
        "moment_one": gaussian(key_of[2], (BLOCKS, BR, F), 0.5, 4.0, ((0, 32), (2, 4)), jnp.float32),
        "moment_two": jnp.clip(jnp.exp(math.log(4.0) - 4.3820266 * jax.random.uniform(key_of[3], (BLOCKS, BR, F), jnp.float32) ** block_levels(key_of[3], (BLOCKS, BR, F), ((0, 32), (2, 4)), -0.2, 0.2)), 0.05, 4.0),
        "context": gaussian(key_of[4], (TOK, HV), 1.0, 6.0, ((0, 32), (1, 4))),
        "out_weight": gaussian(key_of[5], (HV, D), HV ** -0.5, 0.09375, ((0, 4), (1, 32))),
        "hidden": gaussian(key_of[6], (TOK, D), 1.0, 6.0, ((0, 32),)),
        "norm_gain": jnp.clip(1.0 + 0.15 * jax.random.normal(key_of[7], (D,), jnp.float32), 0.25, 1.75),
        "route": with_ends(jax.random.randint(key_of[8], (TOK,), 0, EXPERTS), jax.random.fold_in(key_of[8], 1), 0, EXPERTS - 1).astype(jnp.int32),
        "plan": draw_plan(jax.random.fold_in(key_of[10], 71), 0),
    }


beta_one = 0.9
beta_two = 0.95
bias_one = 1.0 - 0.9 ** 50
bias_two = 1.0 - 0.95 ** 50
learn_rate = 0.0003
decay_rate = 0.1
adam_eps = 1e-08

def reference(master, grad, moment_one, moment_two, context, out_weight, hidden, norm_gain, route, plan):
    gradient = grad.astype(jnp.float32)
    new_first = beta_one * moment_one + (1.0 - beta_one) * gradient
    new_second = beta_two * moment_two + (1.0 - beta_two) * gradient * gradient
    update = new_first / bias_one / (jnp.sqrt(new_second / bias_two) + adam_eps) + decay_rate * master
    new_master = master - learn_rate * update
    cast = new_master.astype(jnp.bfloat16)
    rollout = jnp.take(cast, plan, axis=0)
    attn = jnp.dot(context, out_weight, preferred_element_type=jnp.float32)
    resid = hidden.astype(jnp.float32) + attn
    scale = lax.rsqrt(lax.optimization_barrier(jnp.mean(resid * resid, axis=1, keepdims=True)) + 1e-06)
    normed = (resid * scale * norm_gain[None, :]).astype(jnp.bfloat16)
    weights = cast.reshape(EXPERTS, D, F)

    def one_expert(matrix):
        return jnp.dot(normed, matrix, preferred_element_type=jnp.float32)
    per_expert = lax.map(one_expert, weights)
    select = (route[None, :] == jnp.arange(EXPERTS, dtype=jnp.int32)[:, None]).astype(jnp.float32)
    pre = lax.optimization_barrier(jnp.sum(per_expert * select[:, :, None], axis=0))
    activation = jax.nn.silu(pre).astype(jnp.bfloat16)
    return (new_master, new_first, new_second, rollout, activation)
```

```python
import functools

import jax
import jax.numpy as jnp
from jax import lax
from jax.experimental import pallas as pl
from jax.experimental.pallas import tpu as pltpu
from jax.sharding import PartitionSpec as P

MESH = pl.DeviceIdType.MESH
CAP = 2
N_E = 32
N_T = 4
TOK_DEV = 16
COLS = 224
WIDE = 256
GROUP = 128
FCOL = 512
MSG = 640

beta_one = 0.9
beta_two = 0.95
bias_one = 1.0 - 0.9**50
bias_two = 1.0 - 0.95**50
learn_rate = 0.0003
decay_rate = 0.1
adam_eps = 1e-08


def split_sum(total):
    high = total.astype(jnp.bfloat16)
    low = (total - high.astype(jnp.float32)).astype(jnp.bfloat16)
    return high.astype(jnp.float32), low.astype(jnp.float32)


def decode_kernel(
    ctx, ow, hid, gain, cast, pre_out,
    ctx_all, ow_wide, hid_send, hid_recv, gain_all, part_send, part_recv, part_own, msg, held, pre_send,
    s_ctx, r_ctx, s_hid, r_hid, s_part, r_part, s_msg, r_msg, s_held, r_held, s_pre, r_pre, local_sem,
):
    e = lax.axis_index("expert")
    t = lax.axis_index("tensor")
    y, x, z = e // 8, (e // 2) % 4, e % 2

    barrier = pltpu.get_barrier_semaphore()

    @pl.loop(1, N_E)
    def _(i):
        pl.semaphore_signal(barrier, 1, device_id=((e + i) % N_E, t), device_id_type=MESH)

    for j in range(1, N_T):
        pl.semaphore_signal(barrier, 1, device_id=(e, (t + j) % N_T), device_id_type=MESH)
    pl.semaphore_wait(barrier, N_E - 1 + N_T - 1)

    def ctx_copy(i):
        return pltpu.make_async_remote_copy(
            ctx, ctx_all.at[e], s_ctx.at[i], r_ctx.at[i], device_id=((e + i) % N_E, t), device_id_type=MESH
        )

    @pl.loop(1, N_E)
    def _(i):
        ctx_copy(i).start()

    ctx_all[e] = ctx[...]

    spot = x * 2 + z
    sends_hidden = y == t

    def hid_copy(i):
        return pltpu.make_async_remote_copy(
            hid_send.at[(e + i) % N_E], hid_recv.at[spot], s_hid.at[i], r_hid.at[spot],
            device_id=((e + i) % N_E, t), device_id_type=MESH,
        )

    @pl.when(sends_hidden)
    def _():
        hid_send[...] = jnp.zeros_like(hid_send)
        for g in range(N_E):
            hid_send[g, :, :COLS] = hid[:, g * COLS : (g + 1) * COLS]

        @pl.loop(1, N_E)
        def _(i):
            hid_copy(i).start()

        hid_recv[spot] = hid_send[e]

    gain_all[...] = jnp.zeros_like(gain_all)
    for g in range(N_E):
        gain_all[g, :, :COLS] = gain[:, g * COLS : (g + 1) * COLS]
    ow_wide[...] = jnp.zeros_like(ow_wide)
    ow_wide[:, :COLS] = ow[...]

    @pl.loop(1, N_E)
    def _(i):
        ctx_copy(i).wait_recv()

    def projected(group):
        values = ctx_all[pl.ds(group * 8, 8)].reshape(GROUP, ctx.shape[1])
        return jnp.dot(values, ow_wide[...], preferred_element_type=jnp.float32)

    def part_copy(j):
        return pltpu.make_async_remote_copy(
            part_send.at[j], part_recv.at[j], s_part.at[j], r_part.at[j],
            device_id=(e, (t + j) % N_T), device_id_type=MESH,
        )

    for j in (2, 3, 1):
        part_send[j] = projected((t + j) % N_T).astype(jnp.bfloat16)
        part_copy(j).start()
    part_own[...] = projected(t)

    for q in range(8):
        @pl.when(t * 8 + q != e)
        def _(q=q):
            pltpu.make_async_copy(hid_recv.at[q], hid_recv.at[q], r_hid.at[q]).wait()

    resid = part_own[...] + hid_recv[...].reshape(GROUP, WIDE).astype(jnp.float32)
    for j in (1, 2, 3):
        part_copy(j).wait_recv()
        resid = resid + part_recv[j].astype(jnp.float32)
    high, low = split_sum(jnp.sum(resid * resid, axis=1, keepdims=True))
    lane = lax.broadcasted_iota(jnp.int32, (GROUP, WIDE), 1)
    scaled = resid * gain_all[e]
    scaled = jnp.where(lane == COLS, high, jnp.where(lane == COLS + 1, low, scaled))
    msg[...] = scaled.astype(jnp.bfloat16)

    spot_in = (x % 2) * 2 + z
    my_slice = 2 * x + z

    def msg_copy(k):
        target = k * 8 + 2 * y + x // 2
        return target, pltpu.make_async_remote_copy(
            msg, held.at[t, spot_in], s_msg.at[k], r_msg.at[spot_in], device_id=(target, t), device_id_type=MESH
        )

    for k in range(4):
        target, copy = msg_copy(k)

        @pl.when(target != e)
        def _(copy=copy):
            copy.start()

        @pl.when(target == e)
        def _():
            held[t, spot_in] = msg[...]

    for j in range(4):
        @pl.when(my_slice * 4 + j != e)
        def _(j=j):
            pltpu.make_async_copy(held.at[t, j], held.at[t, j], r_msg.at[j]).wait()

    def held_copy(j):
        return pltpu.make_async_remote_copy(
            held.at[t], held.at[t], s_held.at[j], r_held.at[j], device_id=(e, (t + j) % N_T), device_id_type=MESH
        )

    for j in (2, 3, 1):
        held_copy(j).start()

    def pre_copy(o):
        return pltpu.make_async_remote_copy(
            pre_send.at[o], pre_out.at[e], s_pre.at[o], r_pre.at[e], device_id=(o, t), device_id_type=MESH
        )

    own_copy = pltpu.make_async_copy(pre_send.at[e], pre_out.at[e], local_sem)

    tail_lane = lax.broadcasted_iota(jnp.int32, (GROUP, MSG - FCOL), 1)
    for j in (0, 1, 2, 3):
        if j:
            group = (t + N_T - j) % N_T
            pltpu.make_async_copy(held.at[group], held.at[group], r_held.at[j]).wait()
        else:
            group = t
        weight = cast[...].reshape(896, FCOL)
        total = jnp.zeros((GROUP, FCOL), jnp.float32)
        squares = jnp.zeros((GROUP, 1), jnp.float32)
        for i in range(4):
            block = held[group, i]
            total = total + jnp.dot(
                block[:, :COLS], weight[i * COLS : (i + 1) * COLS], preferred_element_type=jnp.float32
            )
            tail = block[:, GROUP:].astype(jnp.float32)
            squares = squares + jnp.sum(
                jnp.where(tail_lane >= COLS - GROUP, tail, 0.0), axis=1, keepdims=True
            )
        high, low = split_sum(squares)
        extra = jnp.where(tail_lane == 0, high, jnp.where(tail_lane == 1, low, 0.0))
        pre_send[pl.ds(group * 8, 8), :, :FCOL] = total.astype(jnp.bfloat16).reshape(8, TOK_DEV, FCOL)
        pre_send[pl.ds(group * 8, 8), :, FCOL:] = extra.astype(jnp.bfloat16).reshape(8, TOK_DEV, MSG - FCOL)

        @pl.loop(0, 8)
        def _(q, group=group):
            o = group * 8 + q

            @pl.when(o != e)
            def _():
                pre_copy(o).start()

            @pl.when(o == e)
            def _():
                own_copy.start()

    own_copy.wait()

    @pl.loop(1, N_E)
    def _(i):
        source = (e + i) % N_E
        pltpu.make_async_copy(pre_send.at[source], pre_out.at[source], r_pre.at[source]).wait()
        pre_copy(source).wait_send()
        ctx_copy(i).wait_send()

    @pl.when(sends_hidden)
    def _():
        @pl.loop(1, N_E)
        def _(i):
            hid_copy(i).wait_send()

    for j in (1, 2, 3):
        part_copy(j).wait_send()
        held_copy(j).wait_send()
    for k in range(4):
        target, copy = msg_copy(k)

        @pl.when(target != e)
        def _(copy=copy):
            copy.wait_send()


def decode(context, out_weight, hidden, norm_gain, cast):
    vmem = pl.BlockSpec(memory_space=pltpu.VMEM)
    dma = pltpu.SemaphoreType.DMA
    bf16 = jnp.bfloat16
    return pl.pallas_call(
        decode_kernel,
        out_shape=jax.ShapeDtypeStruct((N_E, TOK_DEV, MSG), bf16),
        in_specs=[vmem] * 5,
        out_specs=pl.BlockSpec(memory_space=pl.ANY),
        scratch_shapes=[
            pltpu.VMEM((N_E, TOK_DEV, context.shape[1]), bf16),
            pltpu.VMEM((out_weight.shape[0], WIDE), bf16),
            pltpu.VMEM((N_E, TOK_DEV, WIDE), bf16),
            pltpu.VMEM((8, TOK_DEV, WIDE), bf16),
            pltpu.VMEM((N_E, 1, WIDE), jnp.float32),
            pltpu.VMEM((N_T, GROUP, WIDE), bf16),
            pltpu.VMEM((N_T, GROUP, WIDE), bf16),
            pltpu.VMEM((GROUP, WIDE), jnp.float32),
            pltpu.VMEM((GROUP, WIDE), bf16),
            pltpu.VMEM((N_T, 4, GROUP, WIDE), bf16),
            pltpu.VMEM((N_E, TOK_DEV, MSG), bf16),
            dma((N_E,)), dma((N_E,)), dma((N_E,)), dma((8,)), dma((N_T,)), dma((N_T,)), dma((4,)), dma((4,)),
            dma((N_T,)), dma((N_T,)), dma((N_E,)), dma((N_E,)), dma,
        ],
        compiler_params=pltpu.CompilerParams(
            collective_id=0, has_side_effects=True, vmem_limit_bytes=40 * 2**20
        ),
        cost_estimate=pl.CostEstimate(flops=10**9, bytes_accessed=10**8, transcendentals=0),
        name="decode",
    )(context, out_weight, hidden, norm_gain.reshape(1, -1), cast)


def finish_kernel(partial, route, out):
    expert = route[...]
    pre = jnp.zeros((TOK_DEV, FCOL), jnp.float32)
    squares = jnp.zeros((TOK_DEV, 1), jnp.float32)
    for k in range(4):
        total = jnp.zeros((TOK_DEV, FCOL), jnp.float32)
        for h in range(8):
            total = total + partial[k * 8 + h, :, :FCOL].astype(jnp.float32)
        pre = pre + jnp.where(expert == k, total, 0.0)
    for h in range(8):
        squares = squares + jnp.sum(partial[h, :, FCOL:].astype(jnp.float32), axis=1, keepdims=True)
    pre = pre * lax.rsqrt(squares / (N_E * COLS) + 1e-06)
    out[...] = (pre / (1.0 + jnp.exp(-pre))).astype(jnp.bfloat16)


def finish(partial, route_own):
    return pl.pallas_call(
        finish_kernel, out_shape=jax.ShapeDtypeStruct((TOK_DEV, FCOL), jnp.bfloat16), name="finish"
    )(partial, route_own)


def shards(
    master, grad, moment_one, moment_two, context, out_weight, hidden, norm_gain, route, plan
):
    gradient = grad.astype(jnp.float32)
    new_first = beta_one * moment_one + (1.0 - beta_one) * gradient
    new_second = beta_two * moment_two + (1.0 - beta_two) * gradient * gradient
    update = (
        new_first / bias_one / (jnp.sqrt(new_second / bias_two) + adam_eps) + decay_rate * master
    )
    new_master = master - learn_rate * update
    cast = new_master.astype(jnp.bfloat16)
    owners = lax.axis_size("expert")
    owner_index = lax.axis_index("expert")
    blk_dev = cast.shape[0]
    block_rows = cast.shape[1]
    columns = cast.shape[2]
    slot_count = plan.shape[0] // owners
    table = plan.reshape(owners, slot_count)
    source = table // blk_dev
    local = table % blk_dev
    positions = jnp.arange(slot_count, dtype=jnp.int32)
    same_source = source[:, :, None] == source[:, None, :]
    before = positions[:, None] > positions[None, :]
    rank = jnp.sum((same_source & before[None, :, :]).astype(jnp.int32), axis=2)
    mine = source == owner_index
    hit = mine[:, :, None] & (rank[:, :, None] == jnp.arange(CAP, dtype=jnp.int32)[None, None, :])
    send_index = jnp.sum(hit.astype(jnp.int32) * local[:, :, None], axis=1)
    outgoing = jnp.take(cast, send_index.reshape(owners * CAP), axis=0).reshape(
        owners, CAP, block_rows, columns
    )
    incoming = lax.all_to_all(outgoing, "expert", split_axis=0, concat_axis=0, tiled=True)
    flat_blocks = incoming.reshape(owners * CAP, block_rows, columns)
    wanted = source[owner_index] * CAP + rank[owner_index]
    rollout = jnp.take(flat_blocks, wanted, axis=0)
    partial = decode(context, out_weight, hidden, norm_gain, cast)
    route_own = lax.dynamic_slice(route, (owner_index * TOK_DEV,), (TOK_DEV,)).reshape(TOK_DEV, 1)
    activation = finish(partial, route_own)
    return (new_master, new_first, new_second, rollout, activation)


def solution(mesh):
    return jax.shard_map(
        shards,
        mesh=mesh,
        in_specs=(
            P("expert", None, "tensor"),
            P("expert", None, "tensor"),
            P("expert", None, "tensor"),
            P("expert", None, "tensor"),
            P("expert", "tensor"),
            P("tensor", "expert"),
            P("expert", None),
            P(),
            P(),
            P(),
        ),
        out_specs=(
            P("expert", None, "tensor"),
            P("expert", None, "tensor"),
            P("expert", None, "tensor"),
            P("expert", None, "tensor"),
            P("expert", "tensor"),
        ),
        check_vma=False,
    )
```

```python
import functools

import jax
import jax.numpy as jnp
from jax import lax
from jax.experimental import pallas as pl
from jax.experimental.pallas import tpu as pltpu
from jax.sharding import PartitionSpec as P

MESH = pl.DeviceIdType.MESH
CAP = 2
N_E = 32
N_T = 4
TOK_DEV = 16
COLS = 224
WIDE = 256
GROUP = 128
FCOL = 512
MSG = 640
HALF = 64

beta_one = 0.9
beta_two = 0.95
bias_one = 1.0 - 0.9**50
bias_two = 1.0 - 0.95**50
learn_rate = 0.0003
decay_rate = 0.1
adam_eps = 1e-08


def split_sum(total):
    high = total.astype(jnp.bfloat16)
    low = (total - high.astype(jnp.float32)).astype(jnp.bfloat16)
    return high.astype(jnp.float32), low.astype(jnp.float32)


def step_kernel(
    ctx, ow, hid, gain, table, cast, pre_out, roll_a, roll_b,
    ctx_all, ow_wide, hid_send, hid_recv, gain_all, part_send, part_recv, part_own, msg, held, pre_send, *rest
):
    near = (rest[0:7], rest[7:14])
    picked = rest[14:16]
    (
        s_ctx, r_ctx, s_hid, r_hid, s_part, r_part, s_msg, r_msg, s_held, r_held, s_pre, r_pre, local_sem,
        s_near, r_near, s_pick, r_pick, l_pick,
    ) = rest[16:]
    roll = (roll_a, roll_b)
    e = lax.axis_index("expert")
    t = lax.axis_index("tensor")
    y, x, z = e // 8, (e // 2) % 4, e % 2

    barrier = pltpu.get_barrier_semaphore()

    @pl.loop(1, N_E)
    def _(i):
        pl.semaphore_signal(barrier, 1, device_id=((e + i) % N_E, t), device_id_type=MESH)

    for j in range(1, N_T):
        pl.semaphore_signal(barrier, 1, device_id=(e, (t + j) % N_T), device_id_type=MESH)
    pl.semaphore_wait(barrier, N_E - 1 + N_T - 1)

    def at(dy, dx, dz):
        return ((y + dy) % 4) * 8 + ((x + dx) % 4) * 2 + (z + dz) % 2

    def gather_to(half, d, dz=0):
        return at(d, 0, dz) if half == 0 else at(0, d, dz)

    def owner_at(half, d):
        return at(0, d, 0) if half == 0 else at(d, 0, 0)

    def own_rows(half):
        return cast.at[:, pl.ds(half * HALF, HALF)]

    def near_copy(half, step):
        source, place, target = {
            "z": (None, 1, gather_to(half, 0, 1)),
            "own+": (None, 6, gather_to(half, 1)),
            "own-": (None, 2, gather_to(half, 3)),
            "z+": (1, 7, gather_to(half, 1)),
            "z-": (1, 3, gather_to(half, 3)),
            "on+": (6, 4, gather_to(half, 1)),
            "on-": (3, 5, gather_to(half, 3)),
        }[step]
        index = half * 8 + place
        return pltpu.make_async_remote_copy(
            own_rows(half) if source is None else near[half][source - 1], near[half][place - 1],
            s_near.at[index], r_near.at[index], device_id=(target, t), device_id_type=MESH,
        )

    def pick_copy(half, g, d):
        index = half * 24 + g * 3 + d - 1
        return pltpu.make_async_remote_copy(
            picked[half].at[g, d], roll[half].at[4 - d, g], s_pick.at[index], r_pick.at[index],
            device_id=(owner_at(half, d), t), device_id_type=MESH,
        )

    def keep_copy(half, g):
        return pltpu.make_async_copy(picked[half].at[g, 0], roll[half].at[0, g], l_pick.at[half * 8 + g])

    def pick(half, g):
        source = gather_to(half, g // 2, g % 2)
        for d in (1, 3, 2, 0):
            owner = owner_at(half, d)
            for r in range(CAP):
                block = table[(source * N_E + owner) * CAP + r]
                if g == 0:
                    picked[half][g, d, r] = cast[block, pl.ds(half * HALF, HALF)]
                else:
                    picked[half][g, d, r] = near[half][g - 1][block]
            if d:
                pick_copy(half, g, d).start()
            else:
                keep_copy(half, g).start()

    STEPS = ("z", "own+", "own-", "z+", "z-", "on+", "on-")

    def ctx_copy(i):
        return pltpu.make_async_remote_copy(
            ctx, ctx_all.at[e], s_ctx.at[i], r_ctx.at[i], device_id=((e + i) % N_E, t), device_id_type=MESH
        )

    def ctx_start():
        @pl.loop(1, N_E)
        def _(i):
            ctx_copy(i).start()

        ctx_all[e] = ctx[...]

    spot = x * 2 + z
    sends_hidden = y == t

    def hid_copy(i):
        return pltpu.make_async_remote_copy(
            hid_send.at[(e + i) % N_E], hid_recv.at[spot], s_hid.at[i], r_hid.at[spot],
            device_id=((e + i) % N_E, t), device_id_type=MESH,
        )

    def hid_start():
        @pl.when(sends_hidden)
        def _():
            hid_send[...] = jnp.zeros_like(hid_send)
            for g in range(N_E):
                hid_send[g, :, :COLS] = hid[:, g * COLS : (g + 1) * COLS]

            @pl.loop(1, N_E)
            def _(i):
                hid_copy(i).start()

            hid_recv[spot] = hid_send[e]

    def prepare():
        gain_all[...] = jnp.zeros_like(gain_all)
        for g in range(N_E):
            gain_all[g, :, :COLS] = gain[:, g * COLS : (g + 1) * COLS]
        ow_wide[...] = jnp.zeros_like(ow_wide)
        ow_wide[:, :COLS] = ow[...]

    def ctx_wait():
        @pl.loop(1, N_E)
        def _(i):
            ctx_copy(i).wait_recv()

    def projected(group):
        values = ctx_all[pl.ds(group * 8, 8)].reshape(GROUP, ctx.shape[1])
        return jnp.dot(values, ow_wide[...], preferred_element_type=jnp.float32)

    def part_copy(j):
        return pltpu.make_async_remote_copy(
            part_send.at[j], part_recv.at[j], s_part.at[j], r_part.at[j],
            device_id=(e, (t + j) % N_T), device_id_type=MESH,
        )

    def project():
        for j in (2, 3, 1):
            part_send[j] = projected((t + j) % N_T).astype(jnp.bfloat16)
            part_copy(j).start()
        part_own[...] = projected(t)

    def residual():
        for q in range(8):
            @pl.when(t * 8 + q != e)
            def _(q=q):
                pltpu.make_async_copy(hid_recv.at[q], hid_recv.at[q], r_hid.at[q]).wait()

        resid = part_own[...] + hid_recv[...].reshape(GROUP, WIDE).astype(jnp.float32)
        for j in (1, 2, 3):
            part_copy(j).wait_recv()
            resid = resid + part_recv[j].astype(jnp.float32)
        high, low = split_sum(jnp.sum(resid * resid, axis=1, keepdims=True))
        lane = lax.broadcasted_iota(jnp.int32, (GROUP, WIDE), 1)
        scaled = resid * gain_all[e]
        scaled = jnp.where(lane == COLS, high, jnp.where(lane == COLS + 1, low, scaled))
        msg[...] = scaled.astype(jnp.bfloat16)

    spot_in = (x % 2) * 2 + z
    my_slice = 2 * x + z

    def msg_copy(k):
        target = k * 8 + 2 * y + x // 2
        return target, pltpu.make_async_remote_copy(
            msg, held.at[t, spot_in], s_msg.at[k], r_msg.at[spot_in], device_id=(target, t), device_id_type=MESH
        )

    def msg_start():
        for k in range(4):
            target, copy = msg_copy(k)

            @pl.when(target != e)
            def _(copy=copy):
                copy.start()

            @pl.when(target == e)
            def _():
                held[t, spot_in] = msg[...]

    def msg_wait():
        for j in range(4):
            @pl.when(my_slice * 4 + j != e)
            def _(j=j):
                pltpu.make_async_copy(held.at[t, j], held.at[t, j], r_msg.at[j]).wait()

    def held_copy(j):
        return pltpu.make_async_remote_copy(
            held.at[t], held.at[t], s_held.at[j], r_held.at[j], device_id=(e, (t + j) % N_T), device_id_type=MESH
        )

    def held_start():
        for j in (2, 3, 1):
            held_copy(j).start()

    def pre_copy(o):
        return pltpu.make_async_remote_copy(
            pre_send.at[o], pre_out.at[e], s_pre.at[o], r_pre.at[e], device_id=(o, t), device_id_type=MESH
        )

    own_copy = pltpu.make_async_copy(pre_send.at[e], pre_out.at[e], local_sem)

    tail_lane = lax.broadcasted_iota(jnp.int32, (GROUP, MSG - FCOL), 1)

    def expert_rows(j):
        if j:
            group = (t + N_T - j) % N_T
            pltpu.make_async_copy(held.at[group], held.at[group], r_held.at[j]).wait()
        else:
            group = t
        weight = cast[...].reshape(896, FCOL)
        total = jnp.zeros((GROUP, FCOL), jnp.float32)
        squares = jnp.zeros((GROUP, 1), jnp.float32)
        for i in range(4):
            block = held[group, i]
            total = total + jnp.dot(
                block[:, :COLS], weight[i * COLS : (i + 1) * COLS], preferred_element_type=jnp.float32
            )
            tail = block[:, GROUP:].astype(jnp.float32)
            squares = squares + jnp.sum(
                jnp.where(tail_lane >= COLS - GROUP, tail, 0.0), axis=1, keepdims=True
            )
        high, low = split_sum(squares)
        extra = jnp.where(tail_lane == 0, high, jnp.where(tail_lane == 1, low, 0.0))
        pre_send[pl.ds(group * 8, 8), :, :FCOL] = total.astype(jnp.bfloat16).reshape(8, TOK_DEV, FCOL)
        pre_send[pl.ds(group * 8, 8), :, FCOL:] = extra.astype(jnp.bfloat16).reshape(8, TOK_DEV, MSG - FCOL)

        @pl.loop(0, 8)
        def _(q, group=group):
            o = group * 8 + q

            @pl.when(o != e)
            def _():
                pre_copy(o).start()

            @pl.when(o == e)
            def _():
                own_copy.start()

    def finish_decode():
        own_copy.wait()

        @pl.loop(1, N_E)
        def _(i):
            source = (e + i) % N_E
            pltpu.make_async_copy(pre_send.at[source], pre_out.at[source], r_pre.at[source]).wait()
            pre_copy(source).wait_send()
            ctx_copy(i).wait_send()

        @pl.when(sends_hidden)
        def _():
            @pl.loop(1, N_E)
            def _(i):
                hid_copy(i).wait_send()

        for j in (1, 2, 3):
            part_copy(j).wait_send()
            held_copy(j).wait_send()
        for k in range(4):
            target, copy = msg_copy(k)

            @pl.when(target != e)
            def _(copy=copy):
                copy.wait_send()

    ctx_start()
    near_copy(0, "z").start()
    for half in (0, 1):
        near_copy(half, "own+").start()
        near_copy(half, "own-").start()
    hid_start()
    prepare()
    pick(0, 0)
    pick(1, 0)
    ctx_wait()
    project()
    near_copy(1, "z").start()
    near_copy(0, "z").wait_recv()
    near_copy(0, "z+").start()
    near_copy(0, "z-").start()
    residual()
    msg_start()
    near_copy(1, "z").wait_recv()
    near_copy(1, "z+").start()
    near_copy(1, "z-").start()
    for half in (0, 1):
        near_copy(half, "own+").wait_recv()
        near_copy(half, "on+").start()
    pick(0, 1)
    pick(1, 1)
    msg_wait()
    held_start()
    for half in (0, 1):
        near_copy(half, "z-").wait_recv()
        near_copy(half, "on-").start()
    for half in (0, 1):
        pick(half, 6)
    for half in (0, 1):
        near_copy(half, "own-").wait_recv()
        pick(half, 2)
    expert_rows(0)
    expert_rows(1)
    expert_rows(2)
    expert_rows(3)
    for half in (0, 1):
        pick(half, 3)
    for half in (0, 1):
        near_copy(half, "z+").wait_recv()
        pick(half, 7)
    for half in (0, 1):
        near_copy(half, "on+").wait_recv()
        pick(half, 4)
    for half in (0, 1):
        near_copy(half, "on-").wait_recv()
        pick(half, 5)

    finish_decode()
    for half in (0, 1):
        for step in STEPS:
            near_copy(half, step).wait_send()
        for g in range(8):
            keep_copy(half, g).wait()
            for d in (1, 2, 3):
                pick_copy(half, g, d).wait()


def step(context, out_weight, hidden, norm_gain, table, cast):
    vmem = pl.BlockSpec(memory_space=pltpu.VMEM)
    anywhere = pl.BlockSpec(memory_space=pl.ANY)
    dma = pltpu.SemaphoreType.DMA
    bf16 = jnp.bfloat16
    columns = cast.shape[2]
    rolled = jax.ShapeDtypeStruct((4, 8, CAP, HALF, columns), bf16)
    return pl.pallas_call(
        step_kernel,
        out_shape=(jax.ShapeDtypeStruct((N_E, TOK_DEV, MSG), bf16), rolled, rolled),
        in_specs=[vmem] * 4 + [pl.BlockSpec(memory_space=pltpu.SMEM), vmem],
        out_specs=(anywhere,) * 3,
        scratch_shapes=[
            pltpu.VMEM((N_E, TOK_DEV, context.shape[1]), bf16),
            pltpu.VMEM((out_weight.shape[0], WIDE), bf16),
            pltpu.VMEM((N_E, TOK_DEV, WIDE), bf16),
            pltpu.VMEM((8, TOK_DEV, WIDE), bf16),
            pltpu.VMEM((N_E, 1, WIDE), jnp.float32),
            pltpu.VMEM((N_T, GROUP, WIDE), bf16),
            pltpu.VMEM((N_T, GROUP, WIDE), bf16),
            pltpu.VMEM((GROUP, WIDE), jnp.float32),
            pltpu.VMEM((GROUP, WIDE), bf16),
            pltpu.VMEM((N_T, 4, GROUP, WIDE), bf16),
            pltpu.VMEM((N_E, TOK_DEV, MSG), bf16),
            *[pltpu.VMEM((cast.shape[0], HALF, columns), bf16)] * 14,
            *[pltpu.VMEM((8, 4, CAP, HALF, columns), bf16)] * 2,
            dma((N_E,)), dma((N_E,)), dma((N_E,)), dma((8,)), dma((N_T,)), dma((N_T,)), dma((4,)), dma((4,)),
            dma((N_T,)), dma((N_T,)), dma((N_E,)), dma((N_E,)), dma,
            dma((16,)), dma((16,)), dma((48,)), dma((48,)), dma((16,)),
        ],
        compiler_params=pltpu.CompilerParams(
            collective_id=0, has_side_effects=True, vmem_limit_bytes=48 * 2**20
        ),
        name="step",
    )(context, out_weight, hidden, norm_gain.reshape(1, -1), table, cast)


def finish_kernel(place_a, place_b, partial, route, roll_a, roll_b, out, rollout, stage, in_sems, out_sems):
    def fetch(j, half):
        rolled, place = ((roll_a, place_a), (roll_b, place_b))[half]
        return pltpu.make_async_copy(
            rolled.at[place[j]], stage.at[j, pl.ds(half * HALF, HALF)], in_sems.at[2 * j + half]
        )

    def store(j):
        return pltpu.make_async_copy(stage.at[j], rollout.at[j], out_sems.at[j])

    slots = rollout.shape[0]

    @pl.loop(0, slots)
    def _(j):
        fetch(j, 0).start()
        fetch(j, 1).start()

    expert = route[...]
    pre = jnp.zeros((TOK_DEV, FCOL), jnp.float32)
    squares = jnp.zeros((TOK_DEV, 1), jnp.float32)
    for k in range(4):
        total = jnp.zeros((TOK_DEV, FCOL), jnp.float32)
        for h in range(8):
            total = total + partial[k * 8 + h, :, :FCOL].astype(jnp.float32)
        pre = pre + jnp.where(expert == k, total, 0.0)
    for h in range(8):
        squares = squares + jnp.sum(partial[h, :, FCOL:].astype(jnp.float32), axis=1, keepdims=True)
    pre = pre * lax.rsqrt(squares / (N_E * COLS) + 1e-06)
    out[...] = (pre / (1.0 + jnp.exp(-pre))).astype(jnp.bfloat16)

    @pl.loop(0, slots)
    def _(j):
        fetch(j, 0).wait()
        fetch(j, 1).wait()
        store(j).start()

    @pl.loop(0, slots)
    def _(j):
        store(j).wait()


def finish(place_a, place_b, partial, route_own, roll_a, roll_b):
    vmem = pl.BlockSpec(memory_space=pltpu.VMEM)
    smem = pl.BlockSpec(memory_space=pltpu.SMEM)
    anywhere = pl.BlockSpec(memory_space=pl.ANY)
    columns = roll_a.shape[-1]
    slots = place_a.shape[0]
    flat = (4 * 8 * CAP, HALF, columns)
    return pl.pallas_call(
        finish_kernel,
        out_shape=(
            jax.ShapeDtypeStruct((TOK_DEV, FCOL), jnp.bfloat16),
            jax.ShapeDtypeStruct((slots, 2 * HALF, columns), jnp.bfloat16),
        ),
        in_specs=[smem, smem, vmem, vmem, anywhere, anywhere],
        out_specs=(vmem, anywhere),
        scratch_shapes=[
            pltpu.VMEM((slots, 2 * HALF, columns), jnp.bfloat16),
            pltpu.SemaphoreType.DMA((2 * slots,)),
            pltpu.SemaphoreType.DMA((slots,)),
        ],
        compiler_params=pltpu.CompilerParams(vmem_limit_bytes=16 * 2**20),
        name="finish",
    )(place_a, place_b, partial, route_own, roll_a.reshape(flat), roll_b.reshape(flat))


def load_tables(plan, owner_index, blk_dev):
    table = plan.reshape(N_E, -1)
    slot_count = table.shape[1]
    source = table // blk_dev
    local = table % blk_dev
    positions = jnp.arange(slot_count, dtype=jnp.int32)
    same_source = source[:, :, None] == source[:, None, :]
    before = positions[:, None] > positions[None, :]
    rank = jnp.sum((same_source & before[None, :, :]).astype(jnp.int32), axis=2)
    key = source * CAP + rank
    wanted = jnp.arange(N_E * CAP, dtype=jnp.int32).reshape(N_E, 1, CAP, 1)
    sent = jnp.sum(jnp.where(key[None, :, None, :] == wanted, local[None, :, None, :], 0), axis=3)
    mine, my_rank = source[owner_index], rank[owner_index]
    dy = (mine // 8 - owner_index // 8) % 4
    dx = ((mine // 2) % 4 - (owner_index // 2) % 4) % 4
    dz = (mine - owner_index) % 2
    place_a = (dx * 8 + dy * 2 + dz) * CAP + my_rank
    place_b = (dy * 8 + dx * 2 + dz) * CAP + my_rank
    return sent.reshape(-1), place_a, place_b


def shards(
    master, grad, moment_one, moment_two, context, out_weight, hidden, norm_gain, route, plan
):
    gradient = grad.astype(jnp.float32)
    new_first = beta_one * moment_one + (1.0 - beta_one) * gradient
    new_second = beta_two * moment_two + (1.0 - beta_two) * gradient * gradient
    update = (
        new_first / bias_one / (jnp.sqrt(new_second / bias_two) + adam_eps) + decay_rate * master
    )
    new_master = master - learn_rate * update
    cast = new_master.astype(jnp.bfloat16)
    owner_index = lax.axis_index("expert")
    sent, place_a, place_b = load_tables(plan, owner_index, cast.shape[0])
    partial, roll_a, roll_b = step(context, out_weight, hidden, norm_gain, sent, cast)
    route_own = lax.dynamic_slice(route, (owner_index * TOK_DEV,), (TOK_DEV,)).reshape(TOK_DEV, 1)
    activation, rollout = finish(place_a, place_b, partial, route_own, roll_a, roll_b)
    return (new_master, new_first, new_second, rollout, activation)


def solution(mesh):
    return jax.shard_map(
        shards,
        mesh=mesh,
        in_specs=(
            P("expert", None, "tensor"),
            P("expert", None, "tensor"),
            P("expert", None, "tensor"),
            P("expert", None, "tensor"),
            P("expert", "tensor"),
            P("tensor", "expert"),
            P("expert", None),
            P(),
            P(),
            P(),
        ),
        out_specs=(
            P("expert", None, "tensor"),
            P("expert", None, "tensor"),
            P("expert", None, "tensor"),
            P("expert", None, "tensor"),
            P("expert", "tensor"),
        ),
        check_vma=False,
    )
```

```python
import functools

import jax
import jax.numpy as jnp
from jax import lax
from jax.experimental import pallas as pl
from jax.experimental.pallas import tpu as pltpu
from jax.sharding import PartitionSpec as P

MESH = pl.DeviceIdType.MESH
CAP = 2
N_E = 32
N_T = 4
TOK_DEV = 16
COLS = 224
WIDE = 256
GROUP = 128
FCOL = 512
MSG = 640
HALF = 64

beta_one = 0.9
beta_two = 0.95
bias_one = 1.0 - 0.9**50
bias_two = 1.0 - 0.95**50
learn_rate = 0.0003
decay_rate = 0.1
adam_eps = 1e-08


def split_sum(total):
    high = total.astype(jnp.bfloat16)
    low = (total - high.astype(jnp.float32)).astype(jnp.bfloat16)
    return high.astype(jnp.float32), low.astype(jnp.float32)


def parts_of(wide, narrow):
    parts = [(0, True, 0, wide), (1, True, wide, wide)]
    if narrow:
        parts += [(0, False, 2 * wide, narrow), (1, False, 2 * wide + narrow, narrow)]
    return parts


PARTS = parts_of(48, 16)


def step_kernel(
    master, grad, first, second, ctx, ow_in, hid_in, gain_in, plan,
    pre_out, roll, new_master, new_first, new_second,
    table, cast, state_in, grad_in, state_out, sent_index, s_state, s_grad, s_out, s_table,
    ow, hid, gain, s_load, ctx_all,
    ow_wide, hid_send, hid_recv, gain_all, part_send, part_recv, part_own, msg, held, pre_send,
    s_ctx, r_ctx, s_row, r_row, s_hid, r_hid, s_part, r_part, s_msg, r_msg, s_held, r_held, s_pre, r_pre, local_sem,
    s_near, r_near, s_pick, r_pick, *rest
):
    picked = rest[: len(PARTS)]
    near = []
    used = len(PARTS)
    for _, z_first, _, _ in PARTS:
        count = 7 if z_first else 3
        near.append(rest[used : used + count])
        used += count
    e = lax.axis_index("expert")
    t = lax.axis_index("tensor")
    y, x, z = e // 8, (e // 2) % 4, e % 2

    loads = [
        pltpu.make_async_copy(source, target, s_load.at[i])
        for i, (source, target) in enumerate(((ow_in, ow), (hid_in, hid), (gain_in, gain)))
    ]
    for load in loads:
        load.start()

    blocks = cast.shape[0]
    arrays_in, arrays_out = (master, first, second), (new_master, new_first, new_second)

    def state_copy(b, i):
        return pltpu.make_async_copy(arrays_in[i].at[b], state_in.at[i, b], s_state.at[b * 3 + i])

    def grad_copy(b):
        return pltpu.make_async_copy(grad.at[b], grad_in.at[b], s_grad.at[b])

    @pl.loop(0, blocks)
    def _(b):
        for i in range(3):
            state_copy(b, i).start()
        grad_copy(b).start()

    barrier = pltpu.get_barrier_semaphore()

    @pl.loop(1, N_E)
    def _(i):
        pl.semaphore_signal(barrier, 1, device_id=((e + i) % N_E, t), device_id_type=MESH)

    for j in range(1, N_T):
        pl.semaphore_signal(barrier, 1, device_id=(e, (t + j) % N_T), device_id_type=MESH)
    pl.semaphore_wait(barrier, N_E - 1 + N_T - 1)

    def at(dy, dx, dz):
        return ((y + dy) % 4) * 8 + ((x + dx) % 4) * 2 + (z + dz) % 2

    def gather_to(axis, d, dz=0):
        return at(d, 0, dz) if axis == 0 else at(0, d, dz)

    def owner_at(axis, d, dz=0):
        return at(0, d, dz) if axis == 0 else at(d, 0, dz)

    def place_of(p, d, dz):
        return 2 * d + dz if PARTS[p][1] else d

    FIRST, SECOND = (0, 4), (4, 3)

    def step_of(p, step):
        if PARTS[p][1]:
            return {
                "z": (None, 1, 0, 1, None),
                "own+": (None, 6, 1, 0, None),
                "own-": (None, 2, 3, 0, None),
                "z+": (1, 7, 1, 0, None),
                "z-": (1, 3, 3, 0, None),
                "on+": (6, 4, 1, 0, None),
                "on-": (3, 5, 3, 0, None),
            }[step]
        return {
            "own+": (None, 3, 1, 0, None),
            "own-": (None, 1, 3, 0, None),
            "on+": (3, 2, 1, 0, FIRST),
            "on-": (1, 2, 3, 0, SECOND),
        }[step]

    def steps_of(p):
        return ("z", "own+", "own-", "z+", "z-", "on+", "on-") if PARTS[p][1] else ("own+", "own-", "on+", "on-")

    def near_copy(p, step):
        axis, _, row, rows = PARTS[p]
        source, place, d, dz, some = step_of(p, step)
        index = p * 8 + steps_of(p).index(step)
        if source is None:
            piece = cast.at[:, pl.ds(row, rows)]
        else:
            piece = near[p][source - 1]
        target = near[p][place - 1]
        if some is not None:
            piece, target = piece.at[pl.ds(*some)], target.at[pl.ds(*some)]
        return pltpu.make_async_remote_copy(
            piece, target, s_near.at[index], r_near.at[index],
            device_id=(gather_to(axis, d, dz), t), device_id_type=MESH,
        )

    def near_start(*steps):
        for p in range(len(PARTS)):
            for step in steps:
                if step in steps_of(p):
                    near_copy(p, step).start()

    def targets(p):
        return [(d, dz) for dz in ((0,) if PARTS[p][1] else (1, 0)) for d in (1, 3, 2, 0)]

    def pick_copy(p, d, dz, od, odz):
        axis, z_first, row, rows = PARTS[p]
        place = place_of(p, d, dz)
        index = p * 32 + place * len(targets(p)) + targets(p).index((od, odz))
        back = (4 - od) % 4
        slot = roll.at[(back, d, dz + odz) if axis == 0 else (d, back, dz + odz)]
        source, target = picked[p].at[index - p * 32], slot.at[:, pl.ds(row, rows)]
        if (od, odz) == (0, 0):
            return pltpu.make_async_copy(source, target, s_pick.at[index])
        return pltpu.make_async_remote_copy(
            source, target, s_pick.at[index], r_pick.at[index],
            device_id=(owner_at(axis, od, odz), t), device_id_type=MESH,
        )

    def pick(p, d, dz=0):
        axis, _, row, rows = PARTS[p]
        place = place_of(p, d, dz)
        source = gather_to(axis, d, dz)
        for i, (od, odz) in enumerate(targets(p)):
            owner = owner_at(axis, od, odz)
            for r in range(CAP):
                block = table[(owner % 4) * 8 + owner // 4, source * CAP + r]
                if place == 0:
                    found = cast[block, pl.ds(row, rows)]
                else:
                    found = near[p][place - 1][block]
                picked[p][place * len(targets(p)) + i, r] = found
            pick_copy(p, d, dz, od, odz).start()

    def rollout_end():
        for p in range(len(PARTS)):
            for step in steps_of(p):
                near_copy(p, step).wait_send()
            for d in range(4):
                for dz in (0, 1) if PARTS[p][1] else (0,):
                    for od, odz in targets(p):
                        pick_copy(p, d, dz, od, odz).wait()

    def out_copy(b, i):
        return pltpu.make_async_copy(state_out.at[i, b], arrays_out[i].at[b], s_out.at[b * 3 + i])

    def optimize():
        @pl.loop(0, blocks)
        def _(b):
            for i in range(3):
                state_copy(b, i).wait()
            grad_copy(b).wait()

            @pl.loop(0, cast.shape[1] // 16)
            def _(row):
                rows = pl.ds(pl.multiple_of(row * 16, 16), 16)
                weight = state_in[0, b, rows]
                gradient = grad_in[b, rows].astype(jnp.float32)
                one = beta_one * state_in[1, b, rows] + (1.0 - beta_one) * gradient
                two = beta_two * state_in[2, b, rows] + (1.0 - beta_two) * gradient * gradient
                update = (one * (1.0 / bias_one)) / (jnp.sqrt(two * (1.0 / bias_two)) + adam_eps) + decay_rate * weight
                weight = weight - learn_rate * update
                state_out[0, b, rows] = weight
                state_out[1, b, rows] = one
                state_out[2, b, rows] = two
                cast[b, rows] = weight.astype(jnp.bfloat16)

            for i in range(3):
                out_copy(b, i).start()

    def optimize_end():
        @pl.loop(0, blocks)
        def _(b):
            for i in range(3):
                out_copy(b, i).wait()

    table_copy = pltpu.make_async_copy(sent_index, table, s_table)

    def make_table():
        wanted = plan[...]
        source = (wanted * 9363) >> 16
        local = wanted - source * blocks
        lane = lax.broadcasted_iota(jnp.int32, wanted.shape, 1)
        slot = lane % N_E
        rank = jnp.zeros_like(wanted)
        for j in range(1, N_E):
            rank = rank + jnp.where((pltpu.roll(source, j, 1) == source) & (slot >= j), 1, 0)
        key = source * CAP + rank
        for quarter in range(4):
            found = jnp.zeros_like(wanted)
            for j in range(N_E):
                at_lane = quarter * N_E + j
                found = found + jnp.where(key[:, at_lane : at_lane + 1] == lane, local[:, at_lane : at_lane + 1], 0)
            sent_index[pl.ds(quarter * 8, 8)] = found
        table_copy.start()
        table_copy.wait()

    width = ctx_all.shape[-1]

    def ctx_copy(half, i):
        target = gather_to(half, i // 2, i % 2)
        return pltpu.make_async_remote_copy(
            ctx.at[:, pl.ds(half * width, width)], ctx_all.at[half, y, x, z], s_ctx.at[half * 8 + i], r_ctx.at[half * 8 + i],
            device_id=(target, t), device_id_type=MESH,
        )

    def row_copy(half, d):
        rows = ctx_all.at[0, :, x] if half == 0 else ctx_all.at[1, y]
        return pltpu.make_async_remote_copy(
            rows, rows, s_row.at[half * 4 + d], r_row.at[half * 4 + d],
            device_id=(owner_at(half, d), t), device_id_type=MESH,
        )

    def ctx_own(half):
        return pltpu.make_async_copy(
            ctx.at[:, pl.ds(half * width, width)], ctx_all.at[half, y, x, z], s_ctx.at[half * 8]
        )

    def ctx_start():
        for half in (0, 1):
            for i in range(1, 8):
                ctx_copy(half, i).start()
            ctx_own(half).start()

    def row_start():
        for half in (0, 1):
            ctx_own(half).wait()
            for i in range(1, 8):
                ctx_copy(half, i).wait_recv()
            for d in (1, 3, 2):
                row_copy(half, d).start()

    spot = x * 2 + z
    sends_hidden = y == t

    def hid_copy(i):
        return pltpu.make_async_remote_copy(
            hid_send.at[(e + i) % N_E], hid_recv.at[spot], s_hid.at[i], r_hid.at[spot],
            device_id=((e + i) % N_E, t), device_id_type=MESH,
        )

    def hid_start():
        loads[1].wait()

        @pl.when(sends_hidden)
        def _():
            hid_send[...] = jnp.zeros_like(hid_send)
            for g in range(N_E):
                hid_send[g, :, :COLS] = hid[:, g * COLS : (g + 1) * COLS]

            @pl.loop(1, N_E)
            def _(i):
                hid_copy(i).start()

            hid_recv[spot] = hid_send[e]

    def prepare():
        loads[0].wait()
        loads[2].wait()
        gain_all[...] = jnp.zeros_like(gain_all)
        for g in range(N_E):
            gain_all[g, :, :COLS] = gain[:, g * COLS : (g + 1) * COLS]
        ow_wide[...] = jnp.zeros_like(ow_wide)
        ow_wide[:COLS] = ow[...]

    def ctx_wait():
        for half in (0, 1):
            for d in (1, 2, 3):
                row_copy(half, d).wait_recv()

    def projected(group):
        total = jnp.zeros((GROUP, WIDE), jnp.float32)
        for half in (0, 1):
            values = ctx_all[half, group].reshape(GROUP, width)
            weight = ow_wide[:, half * width : (half + 1) * width]
            total = total + lax.dot_general(
                values, weight, (((1,), (1,)), ((), ())), preferred_element_type=jnp.float32
            )
        return total

    def part_copy(j):
        return pltpu.make_async_remote_copy(
            part_send.at[j], part_recv.at[j], s_part.at[j], r_part.at[j],
            device_id=(e, (t + j) % N_T), device_id_type=MESH,
        )

    def project():
        for j in (2, 3, 1):
            part_send[j] = projected((t + j) % N_T).astype(jnp.bfloat16)
            part_copy(j).start()
        part_own[...] = projected(t)

    def residual():
        for q in range(8):
            @pl.when(t * 8 + q != e)
            def _(q=q):
                pltpu.make_async_copy(hid_recv.at[q], hid_recv.at[q], r_hid.at[q]).wait()

        resid = part_own[...] + hid_recv[...].reshape(GROUP, WIDE).astype(jnp.float32)
        for j in (1, 2, 3):
            part_copy(j).wait_recv()
            resid = resid + part_recv[j].astype(jnp.float32)
        high, low = split_sum(jnp.sum(resid * resid, axis=1, keepdims=True))
        lane = lax.broadcasted_iota(jnp.int32, (GROUP, WIDE), 1)
        scaled = resid * gain_all[e]
        scaled = jnp.where(lane == COLS, high, jnp.where(lane == COLS + 1, low, scaled))
        msg[...] = scaled.astype(jnp.bfloat16)

    spot_in = (x % 2) * 2 + z
    my_slice = 2 * x + z

    def msg_copy(k):
        target = k * 8 + 2 * y + x // 2
        return target, pltpu.make_async_remote_copy(
            msg, held.at[t, spot_in], s_msg.at[k], r_msg.at[spot_in], device_id=(target, t), device_id_type=MESH
        )

    def msg_start():
        for k in range(4):
            target, copy = msg_copy(k)

            @pl.when(target != e)
            def _(copy=copy):
                copy.start()

            @pl.when(target == e)
            def _():
                held[t, spot_in] = msg[...]

    def msg_wait():
        for j in range(4):
            @pl.when(my_slice * 4 + j != e)
            def _(j=j):
                pltpu.make_async_copy(held.at[t, j], held.at[t, j], r_msg.at[j]).wait()

    def held_copy(j):
        return pltpu.make_async_remote_copy(
            held.at[t], held.at[t], s_held.at[j], r_held.at[j], device_id=(e, (t + j) % N_T), device_id_type=MESH
        )

    def held_start():
        for j in (2, 3, 1):
            held_copy(j).start()

    def pre_copy(o):
        return pltpu.make_async_remote_copy(
            pre_send.at[o], pre_out.at[e], s_pre.at[o], r_pre.at[e], device_id=(o, t), device_id_type=MESH
        )

    own_copy = pltpu.make_async_copy(pre_send.at[e], pre_out.at[e], local_sem)

    tail_lane = lax.broadcasted_iota(jnp.int32, (GROUP, MSG - FCOL), 1)

    def expert_rows(j):
        if j:
            group = (t + N_T - j) % N_T
            pltpu.make_async_copy(held.at[group], held.at[group], r_held.at[j]).wait()
        else:
            group = t
        weight = cast[...].reshape(896, FCOL)
        total = jnp.zeros((GROUP, FCOL), jnp.float32)
        squares = jnp.zeros((GROUP, 1), jnp.float32)
        for i in range(4):
            block = held[group, i]
            total = total + jnp.dot(
                block[:, :COLS], weight[i * COLS : (i + 1) * COLS], preferred_element_type=jnp.float32
            )
            tail = block[:, GROUP:].astype(jnp.float32)
            squares = squares + jnp.sum(
                jnp.where(tail_lane >= COLS - GROUP, tail, 0.0), axis=1, keepdims=True
            )
        high, low = split_sum(squares)
        extra = jnp.where(tail_lane == 0, high, jnp.where(tail_lane == 1, low, 0.0))
        pre_send[pl.ds(group * 8, 8), :, :FCOL] = total.astype(jnp.bfloat16).reshape(8, TOK_DEV, FCOL)
        pre_send[pl.ds(group * 8, 8), :, FCOL:] = extra.astype(jnp.bfloat16).reshape(8, TOK_DEV, MSG - FCOL)

        @pl.loop(0, 8)
        def _(q, group=group):
            o = group * 8 + q

            @pl.when(o != e)
            def _():
                pre_copy(o).start()

            @pl.when(o == e)
            def _():
                own_copy.start()

    def finish_decode():
        own_copy.wait()

        @pl.loop(1, N_E)
        def _(i):
            source = (e + i) % N_E
            pltpu.make_async_copy(pre_send.at[source], pre_out.at[source], r_pre.at[source]).wait()
            pre_copy(source).wait_send()

        @pl.when(sends_hidden)
        def _():
            @pl.loop(1, N_E)
            def _(i):
                hid_copy(i).wait_send()

        for half in (0, 1):
            for i in range(1, 8):
                ctx_copy(half, i).wait_send()
            for d in (1, 2, 3):
                row_copy(half, d).wait_send()
        for j in (1, 2, 3):
            part_copy(j).wait_send()
            held_copy(j).wait_send()
        for k in range(4):
            target, copy = msg_copy(k)

            @pl.when(target != e)
            def _(copy=copy):
                copy.wait_send()

    n_parts = range(len(PARTS))
    z_parts = [p for p in n_parts if PARTS[p][1]]
    flat_parts = [p for p in n_parts if not PARTS[p][1]]
    ctx_start()
    optimize()
    row_start()
    near_start("z")
    near_start("own+", "own-")
    make_table()
    prepare()
    hid_start()
    for p in z_parts:
        pick(p, 0)
    ctx_wait()
    project()
    for p in flat_parts:
        pick(p, 0)
    for p in z_parts:
        near_copy(p, "z").wait_recv()
        near_copy(p, "z+").start()
        near_copy(p, "z-").start()
    residual()
    msg_start()
    for p in n_parts:
        near_copy(p, "own+").wait_recv()
        near_copy(p, "on+").start()
    for p in flat_parts:
        near_copy(p, "own-").wait_recv()
        near_copy(p, "on-").start()
    for p in z_parts:
        pick(p, 0, 1)
    msg_wait()
    held_start()
    for p in z_parts:
        near_copy(p, "z-").wait_recv()
        near_copy(p, "on-").start()
    for p in z_parts:
        pick(p, 3)
    for p in z_parts:
        near_copy(p, "own-").wait_recv()
        pick(p, 1)
    expert_rows(0)
    expert_rows(1)
    expert_rows(2)
    expert_rows(3)
    for p in flat_parts:
        pick(p, 1)
        pick(p, 3)
    for p in z_parts:
        pick(p, 1, 1)
    for p in z_parts:
        near_copy(p, "z+").wait_recv()
        pick(p, 3, 1)
    for p in flat_parts:
        near_copy(p, "on+").wait_recv()
        near_copy(p, "on-").wait_recv()
        pick(p, 2)
    for p in z_parts:
        near_copy(p, "on+").wait_recv()
        pick(p, 2)
    for p in z_parts:
        near_copy(p, "on-").wait_recv()
        pick(p, 2, 1)

    optimize_end()
    finish_decode()
    rollout_end()


def step(master, grad, first, second, context, out_weight, hidden, norm_gain, plan):
    vmem = pl.BlockSpec(memory_space=pltpu.VMEM)
    anywhere = pl.BlockSpec(memory_space=pl.ANY)
    dma = pltpu.SemaphoreType.DMA
    bf16 = jnp.bfloat16
    blocks, block_rows, columns = master.shape
    state = jax.ShapeDtypeStruct(master.shape, jnp.float32)
    depth = out_weight.shape[0]
    width = hidden.shape[1]
    return pl.pallas_call(
        step_kernel,
        out_shape=(
            jax.ShapeDtypeStruct((N_E, TOK_DEV, MSG), bf16),
            jax.ShapeDtypeStruct((4, 4, 2, CAP, block_rows, columns), bf16),
            state, state, state,
        ),
        in_specs=[anywhere] * 8 + [vmem],
        out_specs=(anywhere,) * 5,
        scratch_shapes=[
            pltpu.SMEM((N_E, 128), jnp.int32),
            pltpu.VMEM(master.shape, bf16),
            pltpu.VMEM((3, *master.shape), jnp.float32),
            pltpu.VMEM(master.shape, bf16),
            pltpu.VMEM((3, *master.shape), jnp.float32),
            pltpu.VMEM((N_E, 128), jnp.int32),
            dma((3 * blocks,)), dma((blocks,)), dma((3 * blocks,)), dma,
            pltpu.VMEM((COLS, depth), bf16),
            pltpu.VMEM((TOK_DEV, width), bf16),
            pltpu.VMEM((1, width), jnp.float32),
            dma((3,)),
            pltpu.VMEM((2, 4, 4, 2, TOK_DEV, depth // 2), bf16),
            pltpu.VMEM((WIDE, depth), bf16),
            pltpu.VMEM((N_E, TOK_DEV, WIDE), bf16),
            pltpu.VMEM((8, TOK_DEV, WIDE), bf16),
            pltpu.VMEM((N_E, 1, WIDE), jnp.float32),
            pltpu.VMEM((N_T, GROUP, WIDE), bf16),
            pltpu.VMEM((N_T, GROUP, WIDE), bf16),
            pltpu.VMEM((GROUP, WIDE), jnp.float32),
            pltpu.VMEM((GROUP, WIDE), bf16),
            pltpu.VMEM((N_T, 4, GROUP, WIDE), bf16),
            pltpu.VMEM((N_E, TOK_DEV, MSG), bf16),
            dma((16,)), dma((16,)), dma((8,)), dma((8,)),
            dma((N_E,)), dma((8,)), dma((N_T,)), dma((N_T,)), dma((4,)), dma((4,)),
            dma((N_T,)), dma((N_T,)), dma((N_E,)), dma((N_E,)), dma,
            dma((32,)), dma((32,)), dma((128,)), dma((128,)),
            *[pltpu.VMEM((32, CAP, rows, columns), bf16) for _, _, _, rows in PARTS],
            *[
                pltpu.VMEM((blocks, rows, columns), bf16)
                for _, z_first, _, rows in PARTS
                for _ in range(7 if z_first else 3)
            ],
        ],
        compiler_params=pltpu.CompilerParams(
            collective_id=0, has_side_effects=True, vmem_limit_bytes=56 * 2**20
        ),
        name="step",
    )(
        master, grad, first, second, context, out_weight.T, hidden, norm_gain.reshape(1, -1), plan.reshape(8, 128)
    )


def finish_kernel(
    plan, route, partial_in, roll, master_in, first_in, second_in,
    out, rollout, master, first, second,
    stage, state, partial, seen, in_sems, out_sems, state_in_sems, state_out_sems, partial_sem,
):
    e = lax.axis_index("expert")
    slots = rollout.shape[0]
    sources, targets = (master_in, first_in, second_in), (master, first, second)

    def fetch(j, place):
        return pltpu.make_async_copy(roll.at[place], stage.at[j], in_sems.at[j])

    def store(j):
        return pltpu.make_async_copy(stage.at[j], rollout.at[j], out_sems.at[j])

    def state_in(i):
        return pltpu.make_async_copy(sources[i], state.at[i], state_in_sems.at[i])

    def state_out(i):
        return pltpu.make_async_copy(state.at[i], targets[i], state_out_sems.at[i])

    partial_copy = pltpu.make_async_copy(partial_in, partial, partial_sem)
    partial_copy.start()
    for i in range(3):
        state_in(i).start()

    @pl.loop(0, N_E)
    def _(j):
        seen[j] = 0

    @pl.loop(0, slots)
    def _(j):
        source = (plan[e * slots + j] * 9363) >> 16
        rank = seen[source]
        seen[source] = rank + 1
        dy = (source // 8 + 4 - e // 8) % 4
        dx = (source // 2 + 4 - (e // 2) % 4) % 4
        dz = (source + e) % 2
        fetch(j, ((dx * 4 + dy) * 2 + dz) * CAP + rank).start()

    for i in range(3):
        state_in(i).wait()
        state_out(i).start()

    @pl.loop(0, slots)
    def _(j):
        fetch(j, 0).wait()
        store(j).start()

    partial_copy.wait()
    token = lax.broadcasted_iota(jnp.int32, (TOK_DEV, 1), 0)
    expert = jnp.zeros((TOK_DEV, 1), jnp.int32)
    for i in range(TOK_DEV):
        expert = jnp.where(token == i, route[e * TOK_DEV + i], expert)
    pre = jnp.zeros((TOK_DEV, FCOL), jnp.float32)
    squares = jnp.zeros((TOK_DEV, 1), jnp.float32)
    for k in range(4):
        total = jnp.zeros((TOK_DEV, FCOL), jnp.float32)
        for h in range(8):
            total = total + partial[k * 8 + h, :, :FCOL].astype(jnp.float32)
        pre = pre + jnp.where(expert == k, total, 0.0)
    for h in range(8):
        squares = squares + jnp.sum(partial[h, :, FCOL:].astype(jnp.float32), axis=1, keepdims=True)
    pre = pre * lax.rsqrt(squares / (N_E * COLS) + 1e-06)
    out[...] = (pre / (1.0 + jnp.exp(-pre))).astype(jnp.bfloat16)

    @pl.loop(0, slots)
    def _(j):
        store(j).wait()

    for i in range(3):
        state_out(i).wait()


def finish(plan, route, partial, roll, state):
    vmem = pl.BlockSpec(memory_space=pltpu.VMEM)
    smem = pl.BlockSpec(memory_space=pltpu.SMEM)
    anywhere = pl.BlockSpec(memory_space=pl.ANY)
    block_rows, columns = roll.shape[-2:]
    slots = plan.shape[0] // N_E
    shape = jax.ShapeDtypeStruct(state[0].shape, jnp.float32)
    dma = pltpu.SemaphoreType.DMA
    return pl.pallas_call(
        finish_kernel,
        out_shape=(
            jax.ShapeDtypeStruct((TOK_DEV, FCOL), jnp.bfloat16),
            jax.ShapeDtypeStruct((slots, block_rows, columns), jnp.bfloat16),
            shape, shape, shape,
        ),
        in_specs=[smem, smem] + [anywhere] * 5,
        out_specs=(vmem,) + (anywhere,) * 4,
        scratch_shapes=[
            pltpu.VMEM((slots, block_rows, columns), jnp.bfloat16),
            pltpu.VMEM((3, *state[0].shape), jnp.float32),
            pltpu.VMEM(partial.shape, partial.dtype),
            pltpu.SMEM((N_E,), jnp.int32),
            dma((slots,)), dma((slots,)), dma((3,)), dma((3,)), dma,
        ],
        compiler_params=pltpu.CompilerParams(vmem_limit_bytes=56 * 2**20),
        name="finish",
    )(plan, route, partial, roll.reshape(4 * 4 * 2 * CAP, block_rows, columns), *state)


def shards(
    master, grad, moment_one, moment_two, context, out_weight, hidden, norm_gain, route, plan
):
    partial, roll, *state = step(
        master, grad, moment_one, moment_two, context, out_weight, hidden, norm_gain, plan
    )
    activation, rollout, *state = finish(plan, route, partial, roll, state)
    return (*state, rollout, activation)


def solution(mesh):
    return jax.shard_map(
        shards,
        mesh=mesh,
        in_specs=(
            P("expert", None, "tensor"),
            P("expert", None, "tensor"),
            P("expert", None, "tensor"),
            P("expert", None, "tensor"),
            P("expert", "tensor"),
            P("tensor", "expert"),
            P("expert", None),
            P(),
            P(),
            P(),
        ),
        out_specs=(
            P("expert", None, "tensor"),
            P("expert", None, "tensor"),
            P("expert", None, "tensor"),
            P("expert", None, "tensor"),
            P("expert", "tensor"),
        ),
        check_vma=False,
    )
```

```python
import functools

import jax
import jax.numpy as jnp
from jax import lax
from jax.experimental import pallas as pl
from jax.experimental.pallas import tpu as pltpu
from jax.sharding import PartitionSpec as P

MESH = pl.DeviceIdType.MESH
CAP = 2
N_E = 32
N_T = 4
TOK_DEV = 16
COLS = 224
WIDE = 256
GROUP = 128
FCOL = 512
HALF = 64

beta_one = 0.9
beta_two = 0.95
bias_one = 1.0 - 0.9**50
bias_two = 1.0 - 0.95**50
learn_rate = 0.0003
decay_rate = 0.1
adam_eps = 1e-08


def split_sum(total):
    high = total.astype(jnp.bfloat16)
    low = (total - high.astype(jnp.float32)).astype(jnp.bfloat16)
    return high.astype(jnp.float32), low.astype(jnp.float32)


def parts_of(wide, narrow):
    parts = [(0, True, 0, wide), (1, True, wide, wide)]
    if narrow:
        parts += [(0, False, 2 * wide, narrow), (1, False, 2 * wide + narrow, narrow)]
    return parts


PARTS = parts_of(48, 16)
EARLY = 2


def step_kernel(
    master, grad, first, second, ctx, ow_in, hid_in, gain_in, plan,
    pre_out, square_out, roll, new_master, new_first, new_second,
    table, cast, state_in, grad_in, state_out, sent_index, s_state, s_grad, s_out, s_table,
    ow, hid, gain, s_load, ctx_all,
    ow_wide, hid_send, hid_recv, gain_all, part_send, part_recv, part_own, msg, held, pre_send, pair_recv, pair_sum, s_pair, r_pair,
    s_ctx, r_ctx, s_row, r_row, s_hid, r_hid, s_part, r_part, s_lift, r_lift, s_msg, r_msg, s_held, r_held, s_pre, r_pre, local_sem,
    square_send, s_square, r_square, s_near, r_near, s_pick, r_pick, *rest
):
    picked = rest[: len(PARTS)]
    near = []
    used = len(PARTS)
    for _, z_first, _, _ in PARTS:
        count = 7 if z_first else 3
        near.append(rest[used : used + count])
        used += count
    e = lax.axis_index("expert")
    t = lax.axis_index("tensor")
    y, x, z = e // 8, (e // 2) % 4, e % 2

    loads = [
        pltpu.make_async_copy(source, target, s_load.at[i])
        for i, (source, target) in enumerate(((ow_in, ow), (hid_in, hid), (gain_in, gain)))
    ]
    for load in loads:
        load.start()

    blocks = cast.shape[0]
    arrays_in, arrays_out = (master, first, second), (new_master, new_first, new_second)

    def state_copy(b, i):
        return pltpu.make_async_copy(arrays_in[i].at[b], state_in.at[i, b], s_state.at[b * 3 + i])

    def grad_copy(b):
        return pltpu.make_async_copy(grad.at[b], grad_in.at[b], s_grad.at[b])

    @pl.loop(0, blocks)
    def _(b):
        for i in range(3):
            state_copy(b, i).start()
        grad_copy(b).start()

    barrier = pltpu.get_barrier_semaphore()

    @pl.loop(1, N_E)
    def _(i):
        pl.semaphore_signal(barrier, 1, device_id=((e + i) % N_E, t), device_id_type=MESH)

    for j in range(1, N_T):
        pl.semaphore_signal(barrier, 1, device_id=(e, (t + j) % N_T), device_id_type=MESH)
    pl.semaphore_wait(barrier, N_E - 1 + N_T - 1)

    def at(dy, dx, dz):
        return ((y + dy) % 4) * 8 + ((x + dx) % 4) * 2 + (z + dz) % 2

    def gather_to(axis, d, dz=0):
        return at(d, 0, dz) if axis == 0 else at(0, d, dz)

    def owner_at(axis, d, dz=0):
        return at(0, d, dz) if axis == 0 else at(d, 0, dz)

    def place_of(p, d, dz):
        return 2 * d + dz if PARTS[p][1] else d

    FIRST, SECOND = (0, 4), (4, 3)
    HEAD, TAIL = (0, EARLY), (EARLY, blocks - EARLY)

    def step_of(p, step):
        if PARTS[p][1]:
            return {
                "z": (None, 1, 0, 1, HEAD),
                "own+": (None, 6, 1, 0, HEAD),
                "own-": (None, 2, 3, 0, HEAD),
                "z b": (None, 1, 0, 1, TAIL),
                "own+ b": (None, 6, 1, 0, TAIL),
                "own- b": (None, 2, 3, 0, TAIL),
                "z+": (1, 7, 1, 0, None),
                "z-": (1, 3, 3, 0, None),
                "on+": (6, 4, 1, 0, None),
                "on-": (3, 5, 3, 0, None),
            }[step]
        return {
            "own+": (None, 3, 1, 0, HEAD),
            "own-": (None, 1, 3, 0, HEAD),
            "own+ b": (None, 3, 1, 0, TAIL),
            "own- b": (None, 1, 3, 0, TAIL),
            "on+": (3, 2, 1, 0, FIRST),
            "on-": (1, 2, 3, 0, SECOND),
        }[step]

    def steps_of(p):
        shared = ("own+", "own-", "own+ b", "own- b", "on+", "on-")
        return (*shared, "z", "z b", "z+", "z-") if PARTS[p][1] else shared

    def near_copy(p, step):
        axis, _, row, rows = PARTS[p]
        source, place, d, dz, some = step_of(p, step)
        index = p * 10 + steps_of(p).index(step)
        some = pl.ds(*(some or (0, blocks)))
        piece = cast.at[some, pl.ds(row, rows)] if source is None else near[p][source - 1].at[some]
        target = near[p][place - 1].at[some]
        return pltpu.make_async_remote_copy(
            piece, target, s_near.at[index], r_near.at[index],
            device_id=(gather_to(axis, d, dz), t), device_id_type=MESH,
        )

    def near_start(*steps):
        for p in range(len(PARTS)):
            for step in steps:
                if step in steps_of(p):
                    near_copy(p, step).start()

    def near_wait(p, step):
        near_copy(p, step).wait_recv()
        if step + " b" in steps_of(p):
            near_copy(p, step + " b").wait_recv()

    def targets(p):
        return [(d, dz) for dz in ((0,) if PARTS[p][1] else (1, 0)) for d in (1, 3, 2, 0)]

    def pick_copy(p, d, dz, od, odz):
        axis, z_first, row, rows = PARTS[p]
        place = place_of(p, d, dz)
        index = p * 32 + place * len(targets(p)) + targets(p).index((od, odz))
        back = (4 - od) % 4
        slot = roll.at[(back, d, dz + odz) if axis == 0 else (d, back, dz + odz)]
        source, target = picked[p].at[index - p * 32], slot.at[:, pl.ds(row, rows)]
        if (od, odz) == (0, 0):
            return pltpu.make_async_copy(source, target, s_pick.at[index])
        return pltpu.make_async_remote_copy(
            source, target, s_pick.at[index], r_pick.at[index],
            device_id=(owner_at(axis, od, odz), t), device_id_type=MESH,
        )

    def pick(p, d, dz=0):
        axis, _, row, rows = PARTS[p]
        place = place_of(p, d, dz)
        source = gather_to(axis, d, dz)
        for i, (od, odz) in enumerate(targets(p)):
            owner = owner_at(axis, od, odz)
            for r in range(CAP):
                block = table[(owner % 4) * 8 + owner // 4, source * CAP + r]
                if place == 0:
                    found = cast[block, pl.ds(row, rows)]
                else:
                    found = near[p][place - 1][block]
                picked[p][place * len(targets(p)) + i, r] = found
            pick_copy(p, d, dz, od, odz).start()

    def rollout_end():
        for p in range(len(PARTS)):
            for step in steps_of(p):
                near_copy(p, step).wait_send()
            for d in range(4):
                for dz in (0, 1) if PARTS[p][1] else (0,):
                    for od, odz in targets(p):
                        pick_copy(p, d, dz, od, odz).wait()

    def out_copy(b, i):
        return pltpu.make_async_copy(state_out.at[i, b], arrays_out[i].at[b], s_out.at[b * 3 + i])

    def optimize(start, count):
        @pl.loop(start, start + count)
        def _(b):
            for i in range(3):
                state_copy(b, i).wait()
            grad_copy(b).wait()

            @pl.loop(0, cast.shape[1] // 32)
            def _(row):
                rows = pl.ds(pl.multiple_of(row * 32, 32), 32)
                weight = state_in[0, b, rows]
                gradient = grad_in[b, rows].astype(jnp.float32)
                one = beta_one * state_in[1, b, rows] + (1.0 - beta_one) * gradient
                two = beta_two * state_in[2, b, rows] + (1.0 - beta_two) * gradient * gradient
                update = (one * (1.0 / bias_one)) / (jnp.sqrt(two * (1.0 / bias_two)) + adam_eps) + decay_rate * weight
                weight = weight - learn_rate * update
                state_out[0, b, rows] = weight
                state_out[1, b, rows] = one
                state_out[2, b, rows] = two
                cast[b, rows] = weight.astype(jnp.bfloat16)

            for i in range(3):
                out_copy(b, i).start()

    def optimize_end():
        @pl.loop(0, blocks)
        def _(b):
            for i in range(3):
                out_copy(b, i).wait()

    table_copy = pltpu.make_async_copy(sent_index, table, s_table)

    def make_table():
        wanted = plan[...]
        source = (wanted * 9363) >> 16
        local = wanted - source * blocks
        lane = lax.broadcasted_iota(jnp.int32, wanted.shape, 1)
        slot = lane % N_E
        rank = jnp.zeros_like(wanted)
        for j in range(1, N_E):
            rank = rank + jnp.where((pltpu.roll(source, j, 1) == source) & (slot >= j), 1, 0)
        key = source * CAP + rank
        for quarter in range(4):
            found = jnp.zeros_like(wanted)
            for j in range(N_E):
                at_lane = quarter * N_E + j
                found = found + jnp.where(key[:, at_lane : at_lane + 1] == lane, local[:, at_lane : at_lane + 1], 0)
            sent_index[pl.ds(quarter * 8, 8)] = found
        table_copy.start()
        table_copy.wait()

    width = ctx_all.shape[-1]

    def ctx_copy(half, i):
        target = gather_to(half, i // 2, i % 2)
        return pltpu.make_async_remote_copy(
            ctx.at[:, pl.ds(half * width, width)], ctx_all.at[half, y, x, z], s_ctx.at[half * 8 + i], r_ctx.at[half * 8 + i],
            device_id=(target, t), device_id_type=MESH,
        )

    def row_copy(half, d):
        rows = ctx_all.at[0, :, x] if half == 0 else ctx_all.at[1, y]
        return pltpu.make_async_remote_copy(
            rows, rows, s_row.at[half * 4 + d], r_row.at[half * 4 + d],
            device_id=(owner_at(half, d), t), device_id_type=MESH,
        )

    def relay_copy(half, d):
        some = pl.ds(0 if d == 1 else 2, 2)
        rows = ctx_all.at[0, some, (x + 4 - d) % 4] if half == 0 else ctx_all.at[1, (y + 4 - d) % 4, some]
        index = half * 4 + d - 1
        return pltpu.make_async_remote_copy(
            rows, rows, s_row.at[index], r_row.at[index],
            device_id=(owner_at(half, d), t), device_id_type=MESH,
        )

    def ctx_own(half):
        return pltpu.make_async_copy(
            ctx.at[:, pl.ds(half * width, width)], ctx_all.at[half, y, x, z], s_ctx.at[half * 8]
        )

    def ctx_start():
        for half in (0, 1):
            for i in range(1, 8):
                ctx_copy(half, i).start()
            ctx_own(half).start()

    def row_start():
        for half in (0, 1):
            ctx_own(half).wait()
            for i in range(1, 8):
                ctx_copy(half, i).wait_recv()
            for d in (1, 3):
                row_copy(half, d).start()

    def row_on():
        for half in (0, 1):
            for d in (1, 3):
                row_copy(half, d).wait_recv()
                relay_copy(half, d).start()

    spot = x * 2 + z
    sends_hidden = y == t

    def hid_copy(i):
        return pltpu.make_async_remote_copy(
            hid_send.at[(e + i) % N_E], hid_recv.at[spot], s_hid.at[i], r_hid.at[spot],
            device_id=((e + i) % N_E, t), device_id_type=MESH,
        )

    def hid_start():
        loads[1].wait()

        @pl.when(sends_hidden)
        def _():
            hid_send[...] = jnp.zeros_like(hid_send)
            for g in range(N_E):
                hid_send[g, :, :COLS] = hid[:, g * COLS : (g + 1) * COLS]

            @pl.loop(1, N_E)
            def _(i):
                hid_copy(i).start()

            hid_recv[spot] = hid_send[e]

    def prepare():
        loads[0].wait()
        loads[2].wait()
        gain_all[...] = jnp.zeros_like(gain_all)
        for g in range(N_E):
            gain_all[g, :, :COLS] = gain[:, g * COLS : (g + 1) * COLS]
        ow_wide[...] = jnp.zeros_like(ow_wide)
        ow_wide[:COLS] = ow[...]

    def ctx_wait():
        for half in (0, 1):
            for d in (1, 3):
                relay_copy(half, d).wait_recv()

    def projected(group):
        total = jnp.zeros((GROUP, WIDE), jnp.float32)
        for half in (0, 1):
            values = ctx_all[half, group].reshape(GROUP, width)
            weight = ow_wide[:, half * width : (half + 1) * width]
            total = total + lax.dot_general(
                values, weight, (((1,), (1,)), ((), ())), preferred_element_type=jnp.float32
            )
        return total

    def part_copy(j):
        return pltpu.make_async_remote_copy(
            part_send.at[j], part_recv.at[j], s_part.at[j], r_part.at[j],
            device_id=(e, (t + j) % N_T), device_id_type=MESH,
        )

    def project():
        for j in (2, 3, 1):
            part_send[j] = projected((t + j) % N_T).astype(jnp.bfloat16)
            part_copy(j).start()
        part_own[...] = projected(t)

    def residual():
        for q in range(8):
            @pl.when(t * 8 + q != e)
            def _(q=q):
                pltpu.make_async_copy(hid_recv.at[q], hid_recv.at[q], r_hid.at[q]).wait()

        resid = part_own[...] + hid_recv[...].reshape(GROUP, WIDE).astype(jnp.float32)
        for j in (1, 2, 3):
            part_copy(j).wait_recv()
            resid = resid + part_recv[j].astype(jnp.float32)
        high, low = split_sum(jnp.sum(resid * resid, axis=1, keepdims=True))
        lane = lax.broadcasted_iota(jnp.int32, (GROUP, WIDE), 1)
        scaled = resid * gain_all[e]
        scaled = jnp.where(lane == COLS, high, jnp.where(lane == COLS + 1, low, scaled))
        msg[y] = scaled.astype(jnp.bfloat16)

    spot_in = (x % 2) * 2 + z

    def lift_copy(d):
        return pltpu.make_async_remote_copy(
            msg.at[y], msg.at[y], s_lift.at[d], r_lift.at[d], device_id=(at(d, 0, 0), t), device_id_type=MESH
        )

    def msg_copy(column):
        target = y * 8 + column * 2 + x // 2
        return target, pltpu.make_async_remote_copy(
            msg.at[column], held.at[t, spot_in], s_msg.at[column], r_msg.at[spot_in],
            device_id=(target, t), device_id_type=MESH,
        )

    def msg_pass(column):
        target, copy = msg_copy(column)

        @pl.when(target != e)
        def _():
            copy.start()

        @pl.when(target == e)
        def _():
            held[t, spot_in] = msg[column]

    def msg_start():
        for d in (2, 1, 3):
            lift_copy(d).start()
        msg_pass(y)

    def msg_on():
        for d in (1, 3, 2):
            source = (y + 4 - d) % 4
            pltpu.make_async_copy(msg.at[source], msg.at[source], r_lift.at[d]).wait()
            msg_pass(source)

    def msg_wait():
        for j in range(4):
            @pl.when((x != 2 * z + j // 2) | (z != j % 2))
            def _(j=j):
                pltpu.make_async_copy(held.at[t, j], held.at[t, j], r_msg.at[j]).wait()

    other_core = t + 1 - 2 * (t % 2)
    other_chip = (t + 2) % N_T
    far = (other_core + 2) % N_T

    def held_copy(i):
        group, target = ((t, other_chip), (t, other_core), (other_chip, other_core))[i]
        return pltpu.make_async_remote_copy(
            held.at[group], held.at[group], s_held.at[i], r_held.at[i], device_id=(e, target), device_id_type=MESH
        )

    def held_start():
        held_copy(0).start()
        held_copy(1).start()

    def held_on():
        held_copy(0).wait_recv()
        held_copy(2).start()

    def pair_copy(group):
        return pltpu.make_async_remote_copy(
            pre_send.at[pl.ds(group * 4, 4), 1 - z], pair_recv.at[pl.ds(group * 4, 4)],
            s_pair.at[group], r_pair.at[group], device_id=(at(0, 0, 1), t), device_id_type=MESH,
        )

    plane_spot = y * 4 + x

    def pre_copy(o):
        return pltpu.make_async_remote_copy(
            pair_sum.at[o], pre_out.at[plane_spot], s_pre.at[o], r_pre.at[plane_spot],
            device_id=(o * 2 + z, t), device_id_type=MESH,
        )

    own_copy = pltpu.make_async_copy(pair_sum.at[plane_spot], pre_out.at[plane_spot], local_sem.at[0])

    def expert_rows(i):
        group = (t, other_core, other_chip, far)[i]
        if i in (1, 3):
            pltpu.make_async_copy(held.at[group], held.at[group], r_held.at[1 if i == 1 else 2]).wait()
        weight = cast[...].reshape(-1, FCOL)
        total = jnp.zeros((GROUP, FCOL), jnp.float32)
        for j in range(4):
            total = total + jnp.dot(
                held[group, j][:, :COLS], weight[j * COLS : (j + 1) * COLS], preferred_element_type=jnp.float32
            )
        pre_send[pl.ds(group * 4, 4)] = total.astype(jnp.bfloat16).reshape(4, 2, TOK_DEV, FCOL)
        pair_copy(group).start()

    def expert_sums(i):
        group = (t, other_core, other_chip, far)[i]
        pair_copy(group).wait_recv()
        rows = pl.ds(group * 4, 4)
        total = pre_send[rows, z].astype(jnp.float32) + pair_recv[rows].astype(jnp.float32)
        pair_sum[rows] = total.astype(jnp.bfloat16)

        @pl.loop(0, 4)
        def _(q):
            o = group * 4 + q

            @pl.when(o != plane_spot)
            def _():
                pre_copy(o).start()

            @pl.when(o == plane_spot)
            def _():
                own_copy.start()

    def square_copy(q):
        return pltpu.make_async_remote_copy(
            square_send.at[q], square_out.at[spot], s_square.at[q], r_square.at[spot],
            device_id=(y * 8 + q, t), device_id_type=MESH,
        )

    own_squares = pltpu.make_async_copy(square_send.at[spot], square_out.at[spot], local_sem.at[1])

    def squares_start():
        tail_lane = lax.broadcasted_iota(jnp.int32, (GROUP, WIDE - GROUP), 1)
        squares = jnp.zeros((GROUP, 1), jnp.float32)
        for j in range(4):
            tail = held[y, j][:, GROUP:].astype(jnp.float32)
            squares = squares + jnp.sum(jnp.where(tail_lane >= COLS - GROUP, tail, 0.0), axis=1, keepdims=True)
        high, low = split_sum(squares)
        extra = jnp.where(tail_lane == 0, high, jnp.where(tail_lane == 1, low, 0.0))
        square_send[...] = extra.astype(jnp.bfloat16).reshape(square_send.shape)
        for q in range(8):
            @pl.when(q != spot)
            def _(q=q):
                square_copy(q).start()

        own_squares.start()

    def finish_decode():
        own_copy.wait()
        own_squares.wait()
        for q in range(8):
            @pl.when(q != spot)
            def _(q=q):
                pltpu.make_async_copy(square_send.at[q], square_out.at[q], r_square.at[q]).wait()
                square_copy(q).wait_send()

        for group in range(4):
            pair_copy(group).wait_send()

        @pl.loop(1, N_E // 2)
        def _(i):
            source = (plane_spot + i) % (N_E // 2)
            pltpu.make_async_copy(pair_sum.at[source], pre_out.at[source], r_pre.at[source]).wait()
            pre_copy(source).wait_send()

        @pl.when(sends_hidden)
        def _():
            @pl.loop(1, N_E)
            def _(i):
                hid_copy(i).wait_send()

        for half in (0, 1):
            for i in range(1, 8):
                ctx_copy(half, i).wait_send()
            for d in (1, 3):
                row_copy(half, d).wait_send()
                relay_copy(half, d).wait_send()
        for j in (1, 2, 3):
            part_copy(j).wait_send()
            held_copy(j - 1).wait_send()
        for column in range(4):
            target, copy = msg_copy(column)

            @pl.when(target != e)
            def _(copy=copy):
                copy.wait_send()
        for d in (1, 2, 3):
            lift_copy(d).wait_send()

    ctx_start()
    optimize(0, EARLY)
    near_start("z", "own+", "own-")
    optimize(EARLY, blocks - EARLY)
    row_start()
    near_start("z b", "own+ b", "own- b")
    make_table()
    prepare()
    hid_start()
    row_on()
    pick(0, 0)
    pick(1, 0)
    ctx_wait()
    project()
    near_wait(0, "z")
    near_copy(0, "z+").start()
    near_copy(0, "z-").start()
    near_wait(1, "z")
    near_copy(1, "z+").start()
    near_copy(1, "z-").start()
    residual()
    msg_start()
    near_wait(0, "own+")
    near_copy(0, "on+").start()
    near_wait(1, "own+")
    near_copy(1, "on+").start()
    near_wait(2, "own+")
    near_copy(2, "on+").start()
    near_wait(3, "own+")
    near_copy(3, "on+").start()
    near_wait(2, "own-")
    near_copy(2, "on-").start()
    near_wait(3, "own-")
    near_copy(3, "on-").start()
    pick(2, 0)
    pick(3, 0)
    msg_on()
    pick(0, 0, 1)
    pick(1, 0, 1)
    pick(2, 1)
    msg_wait()
    held_start()
    near_wait(0, "z-")
    near_copy(0, "on-").start()
    near_wait(1, "z-")
    near_copy(1, "on-").start()
    pick(0, 3)
    pick(1, 3)
    pick(3, 1)
    held_on()
    near_wait(0, "own-")
    pick(0, 1)
    near_wait(1, "own-")
    pick(1, 1)
    expert_rows(0)
    expert_rows(1)
    expert_rows(2)
    expert_rows(3)
    squares_start()
    pick(0, 1, 1)
    pick(1, 1, 1)
    pick(2, 3)
    expert_sums(0)
    expert_sums(1)
    expert_sums(2)
    expert_sums(3)
    pick(3, 3)
    near_wait(0, "z+")
    pick(0, 3, 1)
    near_wait(1, "z+")
    pick(1, 3, 1)
    near_wait(2, "on+")
    near_wait(2, "on-")
    pick(2, 2)
    near_wait(3, "on+")
    near_wait(3, "on-")
    pick(3, 2)
    near_wait(0, "on+")
    pick(0, 2)
    near_wait(1, "on+")
    pick(1, 2)
    near_wait(0, "on-")
    pick(0, 2, 1)
    near_wait(1, "on-")
    pick(1, 2, 1)
    optimize_end()
    finish_decode()
    rollout_end()


def step(master, grad, first, second, context, out_weight, hidden, norm_gain, plan):
    vmem = pl.BlockSpec(memory_space=pltpu.VMEM)
    anywhere = pl.BlockSpec(memory_space=pl.ANY)
    dma = pltpu.SemaphoreType.DMA
    bf16 = jnp.bfloat16
    blocks, block_rows, columns = master.shape
    state = jax.ShapeDtypeStruct(master.shape, jnp.float32)
    depth = out_weight.shape[0]
    width = hidden.shape[1]
    return pl.pallas_call(
        step_kernel,
        out_shape=(
            jax.ShapeDtypeStruct((N_E // 2, TOK_DEV, FCOL), bf16),
            jax.ShapeDtypeStruct((8, TOK_DEV, GROUP), bf16),
            jax.ShapeDtypeStruct((4, 4, 2, CAP, block_rows, columns), bf16),
            state, state, state,
        ),
        in_specs=[anywhere] * 8 + [vmem],
        out_specs=(anywhere,) * 6,
        scratch_shapes=[
            pltpu.SMEM((N_E, 128), jnp.int32),
            pltpu.VMEM(master.shape, bf16),
            pltpu.VMEM((3, *master.shape), jnp.float32),
            pltpu.VMEM(master.shape, bf16),
            pltpu.VMEM((3, *master.shape), jnp.float32),
            pltpu.VMEM((N_E, 128), jnp.int32),
            dma((3 * blocks,)), dma((blocks,)), dma((3 * blocks,)), dma,
            pltpu.VMEM((COLS, depth), bf16),
            pltpu.VMEM((TOK_DEV, width), bf16),
            pltpu.VMEM((1, width), jnp.float32),
            dma((3,)),
            pltpu.VMEM((2, 4, 4, 2, TOK_DEV, depth // 2), bf16),
            pltpu.VMEM((WIDE, depth), bf16),
            pltpu.VMEM((N_E, TOK_DEV, WIDE), bf16),
            pltpu.VMEM((8, TOK_DEV, WIDE), bf16),
            pltpu.VMEM((N_E, 1, WIDE), jnp.float32),
            pltpu.VMEM((N_T, GROUP, WIDE), bf16),
            pltpu.VMEM((N_T, GROUP, WIDE), bf16),
            pltpu.VMEM((GROUP, WIDE), jnp.float32),
            pltpu.VMEM((4, GROUP, WIDE), bf16),
            pltpu.VMEM((N_T, 4, GROUP, WIDE), bf16),
            pltpu.VMEM((N_E // 2, 2, TOK_DEV, FCOL), bf16),
            pltpu.VMEM((N_E // 2, TOK_DEV, FCOL), bf16),
            pltpu.VMEM((N_E // 2, TOK_DEV, FCOL), bf16),
            dma((4,)), dma((4,)),
            dma((16,)), dma((16,)), dma((8,)), dma((8,)),
            dma((N_E,)), dma((8,)), dma((N_T,)), dma((N_T,)), dma((4,)), dma((4,)), dma((4,)), dma((4,)),
            dma((3,)), dma((3,)), dma((N_E // 2,)), dma((N_E // 2,)), dma((2,)),
            pltpu.VMEM((8, TOK_DEV, GROUP), bf16), dma((8,)), dma((8,)),
            dma((40,)), dma((40,)), dma((128,)), dma((128,)),
            *[pltpu.VMEM((32, CAP, rows, columns), bf16) for _, _, _, rows in PARTS],
            *[
                pltpu.VMEM((blocks, rows, columns), bf16)
                for _, z_first, _, rows in PARTS
                for _ in range(7 if z_first else 3)
            ],
        ],
        compiler_params=pltpu.CompilerParams(
            collective_id=0, has_side_effects=True, vmem_limit_bytes=56 * 2**20
        ),
        name="step",
    )(
        master, grad, first, second, context, out_weight.T, hidden, norm_gain.reshape(1, -1), plan.reshape(8, 128)
    )


def finish_kernel(
    plan_in, route_in, partial_in, squares_in, roll, master_in, first_in, second_in,
    out, rollout, master, first, second,
    plan, route, stage, state, partial, square_parts, seen, in_sems, out_sems, state_in_sems, state_out_sems, decode_sems,
):
    e = lax.axis_index("expert")
    slots = rollout.shape[0]
    sources, targets = (master_in, first_in, second_in), (master, first, second)

    def fetch(j, place):
        return pltpu.make_async_copy(roll.at[place], stage.at[j], in_sems.at[j])

    def store(j):
        return pltpu.make_async_copy(stage.at[j], rollout.at[j], out_sems.at[j])

    def state_in(i):
        return pltpu.make_async_copy(sources[i], state.at[i], state_in_sems.at[i])

    def state_out(i):
        return pltpu.make_async_copy(state.at[i], targets[i], state_out_sems.at[i])

    partial_copy = pltpu.make_async_copy(partial_in, partial, decode_sems.at[0])
    squares_copy = pltpu.make_async_copy(squares_in, square_parts, decode_sems.at[1])
    plan_copy = pltpu.make_async_copy(plan_in, plan, decode_sems.at[2])
    route_copy = pltpu.make_async_copy(route_in, route, decode_sems.at[3])
    plan_copy.start()
    route_copy.start()
    for i in range(3):
        state_in(i).start()

    @pl.loop(0, N_E)
    def _(j):
        seen[j] = 0

    plan_copy.wait()
    route_copy.wait()

    @pl.loop(0, slots)
    def _(j):
        source = (plan[e * slots + j] * 9363) >> 16
        rank = seen[source]
        seen[source] = rank + 1
        dy = (source // 8 + 4 - e // 8) % 4
        dx = (source // 2 + 4 - (e // 2) % 4) % 4
        dz = (source + e) % 2
        fetch(j, ((dx * 4 + dy) * 2 + dz) * CAP + rank).start()

    partial_copy.start()
    squares_copy.start()
    for i in range(3):
        state_in(i).wait()
        state_out(i).start()

    @pl.loop(0, slots)
    def _(j):
        fetch(j, 0).wait()
        store(j).start()

    partial_copy.wait()
    squares_copy.wait()
    token = lax.broadcasted_iota(jnp.int32, (TOK_DEV, 1), 0)
    expert = jnp.zeros((TOK_DEV, 1), jnp.int32)
    for i in range(TOK_DEV):
        expert = jnp.where(token == i, route[e * TOK_DEV + i], expert)
    pre = jnp.zeros((TOK_DEV, FCOL), jnp.float32)
    squares = jnp.zeros((TOK_DEV, 1), jnp.float32)
    for k in range(4):
        total = jnp.zeros((TOK_DEV, FCOL), jnp.float32)
        for h in range(4):
            total = total + partial[k * 4 + h].astype(jnp.float32)
        pre = pre + jnp.where(expert == k, total, 0.0)
    for h in range(8):
        squares = squares + jnp.sum(square_parts[h].astype(jnp.float32), axis=1, keepdims=True)
    pre = pre * lax.rsqrt(squares / (N_E * COLS) + 1e-06)
    out[...] = (pre / (1.0 + jnp.exp(-pre))).astype(jnp.bfloat16)

    @pl.loop(0, slots)
    def _(j):
        store(j).wait()

    for i in range(3):
        state_out(i).wait()


def finish(plan, route, partial, squares, roll, state):
    vmem = pl.BlockSpec(memory_space=pltpu.VMEM)
    anywhere = pl.BlockSpec(memory_space=pl.ANY)
    block_rows, columns = roll.shape[-2:]
    slots = plan.shape[0] // N_E
    shape = jax.ShapeDtypeStruct(state[0].shape, jnp.float32)
    dma = pltpu.SemaphoreType.DMA
    return pl.pallas_call(
        finish_kernel,
        out_shape=(
            jax.ShapeDtypeStruct((TOK_DEV, FCOL), jnp.bfloat16),
            jax.ShapeDtypeStruct((slots, block_rows, columns), jnp.bfloat16),
            shape, shape, shape,
        ),
        in_specs=[anywhere] * 8,
        out_specs=(vmem,) + (anywhere,) * 4,
        scratch_shapes=[
            pltpu.SMEM(plan.shape, jnp.int32),
            pltpu.SMEM(route.shape, jnp.int32),
            pltpu.VMEM((slots, block_rows, columns), jnp.bfloat16),
            pltpu.VMEM((3, *state[0].shape), jnp.float32),
            pltpu.VMEM(partial.shape, partial.dtype),
            pltpu.VMEM(squares.shape, squares.dtype),
            pltpu.SMEM((N_E,), jnp.int32),
            dma((slots,)), dma((slots,)), dma((3,)), dma((3,)), dma((4,)),
        ],
        compiler_params=pltpu.CompilerParams(vmem_limit_bytes=56 * 2**20),
        name="finish",
    )(plan, route, partial, squares, roll.reshape(4 * 4 * 2 * CAP, block_rows, columns), *state)


def shards(
    master, grad, moment_one, moment_two, context, out_weight, hidden, norm_gain, route, plan
):
    partial, squares, roll, *state = step(
        master, grad, moment_one, moment_two, context, out_weight, hidden, norm_gain, plan
    )
    activation, rollout, *state = finish(plan, route, partial, squares, roll, state)
    return (*state, rollout, activation)


def solution(mesh):
    return jax.shard_map(
        shards,
        mesh=mesh,
        in_specs=(
            P("expert", None, "tensor"),
            P("expert", None, "tensor"),
            P("expert", None, "tensor"),
            P("expert", None, "tensor"),
            P("expert", "tensor"),
            P("tensor", "expert"),
            P("expert", None),
            P(),
            P(),
            P(),
        ),
        out_specs=(
            P("expert", None, "tensor"),
            P("expert", None, "tensor"),
            P("expert", None, "tensor"),
            P("expert", None, "tensor"),
            P("expert", "tensor"),
        ),
        check_vma=False,
    )
```

```python
import functools

import jax
import jax.numpy as jnp
from jax import lax
from jax.experimental import pallas as pl
from jax.experimental.pallas import tpu as pltpu
from jax.sharding import PartitionSpec as P

MESH = pl.DeviceIdType.MESH
CAP = 2
N_E = 32
N_T = 4
TOK_DEV = 16
COLS = 224
WIDE = 256
GROUP = 128
FCOL = 512
HALF = 64

beta_one = 0.9
beta_two = 0.95
bias_one = 1.0 - 0.9**50
bias_two = 1.0 - 0.95**50
learn_rate = 0.0003
decay_rate = 0.1
adam_eps = 1e-08


def split_sum(total):
    high = total.astype(jnp.bfloat16)
    low = (total - high.astype(jnp.float32)).astype(jnp.bfloat16)
    return high.astype(jnp.float32), low.astype(jnp.float32)


def parts_of(wide, narrow):
    parts = [(0, True, 0, wide), (1, True, wide, wide)]
    if narrow:
        parts += [(0, False, 2 * wide, narrow), (1, False, 2 * wide + narrow, narrow)]
    return parts


PARTS = parts_of(48, 16)
EARLY = 2


def step_kernel(
    master, grad, first, second, ctx, ow_in, hid_in, gain_in, plan_in,
    pre_out, square_out, roll, new_master, new_first, new_second,
    table, cast, state_in, grad_in, state_out, sent_index, s_state, s_grad, s_out, s_table,
    ow, hid, gain, plan, s_load, ctx_all,
    ow_wide, hid_send, hid_recv, gain_all, part_send, part_recv, part_own, msg, held, pre_send, pair_recv, pair_sum, s_pair, r_pair,
    s_ctx, r_ctx, s_row, r_row, s_hid, r_hid, s_part, r_part, s_lift, r_lift, s_msg, r_msg, s_held, r_held, s_pre, r_pre, local_sem,
    square_send, s_square, r_square, s_near, r_near, s_pick, r_pick, *rest
):
    picked = rest[: len(PARTS)]
    near = []
    used = len(PARTS)
    for _, z_first, _, _ in PARTS:
        count = 7 if z_first else 3
        near.append(rest[used : used + count])
        used += count
    e = lax.axis_index("expert")
    t = lax.axis_index("tensor")
    y, x, z = e // 8, (e // 2) % 4, e % 2

    barrier = pltpu.get_barrier_semaphore()

    @pl.loop(1, N_E)
    def _(i):
        pl.semaphore_signal(barrier, 1, device_id=((e + i) % N_E, t), device_id_type=MESH)

    for j in range(1, N_T):
        pl.semaphore_signal(barrier, 1, device_id=(e, (t + j) % N_T), device_id_type=MESH)

    loads = [
        pltpu.make_async_copy(source, target, s_load.at[i])
        for i, (source, target) in enumerate(((ow_in, ow), (hid_in, hid), (gain_in, gain), (plan_in, plan)))
    ]
    for load in loads:
        load.start()

    blocks = cast.shape[0]
    arrays_in, arrays_out = (master, first, second), (new_master, new_first, new_second)

    def state_copy(b, i):
        return pltpu.make_async_copy(arrays_in[i].at[b], state_in.at[i, b], s_state.at[b * 3 + i])

    def grad_copy(b):
        return pltpu.make_async_copy(grad.at[b], grad_in.at[b], s_grad.at[b])

    @pl.loop(0, blocks)
    def _(b):
        for i in range(3):
            state_copy(b, i).start()
        grad_copy(b).start()

    def barrier_wait():
        pl.semaphore_wait(barrier, N_E - 1 + N_T - 1)

    def at(dy, dx, dz):
        return ((y + dy) % 4) * 8 + ((x + dx) % 4) * 2 + (z + dz) % 2

    def gather_to(axis, d, dz=0):
        return at(d, 0, dz) if axis == 0 else at(0, d, dz)

    def owner_at(axis, d, dz=0):
        return at(0, d, dz) if axis == 0 else at(d, 0, dz)

    def place_of(p, d, dz):
        return 2 * d + dz if PARTS[p][1] else d

    FIRST, SECOND = (0, 4), (4, 3)
    HEAD, TAIL = (0, EARLY), (EARLY, blocks - EARLY)

    def step_of(p, step):
        if PARTS[p][1]:
            return {
                "z": (None, 1, 0, 1, HEAD),
                "own+": (None, 6, 1, 0, HEAD),
                "own-": (None, 2, 3, 0, HEAD),
                "z b": (None, 1, 0, 1, TAIL),
                "own+ b": (None, 6, 1, 0, TAIL),
                "own- b": (None, 2, 3, 0, TAIL),
                "z+": (1, 7, 1, 0, None),
                "z-": (1, 3, 3, 0, None),
                "on+": (6, 4, 1, 0, None),
                "on-": (3, 5, 3, 0, None),
            }[step]
        return {
            "own+": (None, 3, 1, 0, HEAD),
            "own-": (None, 1, 3, 0, HEAD),
            "own+ b": (None, 3, 1, 0, TAIL),
            "own- b": (None, 1, 3, 0, TAIL),
            "on+": (3, 2, 1, 0, FIRST),
            "on-": (1, 2, 3, 0, SECOND),
        }[step]

    def steps_of(p):
        shared = ("own+", "own-", "own+ b", "own- b", "on+", "on-")
        return (*shared, "z", "z b", "z+", "z-") if PARTS[p][1] else shared

    def near_copy(p, step):
        axis, _, row, rows = PARTS[p]
        source, place, d, dz, some = step_of(p, step)
        index = p * 10 + steps_of(p).index(step)
        some = pl.ds(*(some or (0, blocks)))
        piece = cast.at[some, pl.ds(row, rows)] if source is None else near[p][source - 1].at[some]
        target = near[p][place - 1].at[some]
        return pltpu.make_async_remote_copy(
            piece, target, s_near.at[index], r_near.at[index],
            device_id=(gather_to(axis, d, dz), t), device_id_type=MESH,
        )

    def near_start(*steps):
        for p in range(len(PARTS)):
            for step in steps:
                if step in steps_of(p):
                    near_copy(p, step).start()

    def near_wait(p, step):
        near_copy(p, step).wait_recv()
        if step + " b" in steps_of(p):
            near_copy(p, step + " b").wait_recv()

    def targets(p):
        return [(d, dz) for dz in ((0,) if PARTS[p][1] else (1, 0)) for d in (1, 3, 2, 0)]

    def pick_copy(p, d, dz, od, odz):
        axis, z_first, row, rows = PARTS[p]
        place = place_of(p, d, dz)
        index = p * 32 + place * len(targets(p)) + targets(p).index((od, odz))
        back = (4 - od) % 4
        slot = roll.at[(back, d, dz + odz) if axis == 0 else (d, back, dz + odz)]
        source, target = picked[p].at[index - p * 32], slot.at[:, pl.ds(row, rows)]
        if (od, odz) == (0, 0):
            return pltpu.make_async_copy(source, target, s_pick.at[index])
        return pltpu.make_async_remote_copy(
            source, target, s_pick.at[index], r_pick.at[index],
            device_id=(owner_at(axis, od, odz), t), device_id_type=MESH,
        )

    def pick(p, d, dz=0):
        axis, _, row, rows = PARTS[p]
        place = place_of(p, d, dz)
        source = gather_to(axis, d, dz)
        for i, (od, odz) in enumerate(targets(p)):
            owner = owner_at(axis, od, odz)
            for r in range(CAP):
                block = table[(owner % 4) * 8 + owner // 4, source * CAP + r]
                if place == 0:
                    found = cast[block, pl.ds(row, rows)]
                else:
                    found = near[p][place - 1][block]
                picked[p][place * len(targets(p)) + i, r] = found
            pick_copy(p, d, dz, od, odz).start()

    def rollout_end():
        for p in range(len(PARTS)):
            for step in steps_of(p):
                near_copy(p, step).wait_send()
            for d in range(4):
                for dz in (0, 1) if PARTS[p][1] else (0,):
                    for od, odz in targets(p):
                        pick_copy(p, d, dz, od, odz).wait()

    def out_copy(b, i):
        return pltpu.make_async_copy(state_out.at[i, b], arrays_out[i].at[b], s_out.at[b * 3 + i])

    def optimize(start, count):
        @pl.loop(start, start + count)
        def _(b):
            for i in range(3):
                state_copy(b, i).wait()
            grad_copy(b).wait()

            @pl.loop(0, cast.shape[1] // 32)
            def _(row):
                rows = pl.ds(pl.multiple_of(row * 32, 32), 32)
                weight = state_in[0, b, rows]
                gradient = grad_in[b, rows].astype(jnp.float32)
                one = beta_one * state_in[1, b, rows] + (1.0 - beta_one) * gradient
                two = beta_two * state_in[2, b, rows] + (1.0 - beta_two) * gradient * gradient
                update = (one * (1.0 / bias_one)) / (jnp.sqrt(two * (1.0 / bias_two)) + adam_eps) + decay_rate * weight
                weight = weight - learn_rate * update
                state_out[0, b, rows] = weight
                state_out[1, b, rows] = one
                state_out[2, b, rows] = two
                cast[b, rows] = weight.astype(jnp.bfloat16)

            for i in range(3):
                out_copy(b, i).start()

    def optimize_end():
        @pl.loop(0, blocks)
        def _(b):
            for i in range(3):
                out_copy(b, i).wait()

    table_copy = pltpu.make_async_copy(sent_index, table, s_table)

    def make_table():
        loads[3].wait()
        wanted = plan[...]
        source = (wanted * 9363) >> 16
        local = wanted - source * blocks
        lane = lax.broadcasted_iota(jnp.int32, wanted.shape, 1)
        slot = lane % N_E
        rank = jnp.zeros_like(wanted)
        for j in range(1, N_E):
            rank = rank + jnp.where((pltpu.roll(source, j, 1) == source) & (slot >= j), 1, 0)
        key = source * CAP + rank
        for quarter in range(4):
            found = jnp.zeros_like(wanted)
            for j in range(N_E):
                at_lane = quarter * N_E + j
                found = found + jnp.where(key[:, at_lane : at_lane + 1] == lane, local[:, at_lane : at_lane + 1], 0)
            sent_index[pl.ds(quarter * 8, 8)] = found
        table_copy.start()
        table_copy.wait()

    width = ctx_all.shape[-1]

    def ctx_copy(half, i):
        target = gather_to(half, i // 2, i % 2)
        return pltpu.make_async_remote_copy(
            ctx.at[:, pl.ds(half * width, width)], ctx_all.at[half, y, x, z], s_ctx.at[half * 8 + i], r_ctx.at[half * 8 + i],
            device_id=(target, t), device_id_type=MESH,
        )

    def row_copy(half, d):
        rows = ctx_all.at[0, :, x] if half == 0 else ctx_all.at[1, y]
        return pltpu.make_async_remote_copy(
            rows, rows, s_row.at[half * 4 + d], r_row.at[half * 4 + d],
            device_id=(owner_at(half, d), t), device_id_type=MESH,
        )

    def relay_copy(half, d):
        some = pl.ds(0 if d == 1 else 2, 2)
        rows = ctx_all.at[0, some, (x + 4 - d) % 4] if half == 0 else ctx_all.at[1, (y + 4 - d) % 4, some]
        index = half * 4 + d - 1
        return pltpu.make_async_remote_copy(
            rows, rows, s_row.at[index], r_row.at[index],
            device_id=(owner_at(half, d), t), device_id_type=MESH,
        )

    def ctx_own(half):
        return pltpu.make_async_copy(
            ctx.at[:, pl.ds(half * width, width)], ctx_all.at[half, y, x, z], s_ctx.at[half * 8]
        )

    def ctx_start():
        for half in (0, 1):
            for i in range(1, 8):
                ctx_copy(half, i).start()
            ctx_own(half).start()

    def row_start():
        for half in (0, 1):
            ctx_own(half).wait()
            for i in range(1, 8):
                ctx_copy(half, i).wait_recv()
            for d in (1, 3):
                row_copy(half, d).start()

    def row_on():
        for half in (0, 1):
            for d in (1, 3):
                row_copy(half, d).wait_recv()
                relay_copy(half, d).start()

    spot = x * 2 + z
    sends_hidden = y == t

    def hid_copy(i):
        return pltpu.make_async_remote_copy(
            hid_send.at[(e + i) % N_E], hid_recv.at[spot], s_hid.at[i], r_hid.at[spot],
            device_id=((e + i) % N_E, t), device_id_type=MESH,
        )

    def hid_start():
        loads[1].wait()

        @pl.when(sends_hidden)
        def _():
            hid_send[...] = jnp.zeros_like(hid_send)
            for g in range(N_E):
                hid_send[g, :, :COLS] = hid[:, g * COLS : (g + 1) * COLS]

            @pl.loop(1, N_E)
            def _(i):
                hid_copy(i).start()

            hid_recv[spot] = hid_send[e]

    def prepare():
        loads[0].wait()
        loads[2].wait()
        gain_all[...] = jnp.zeros_like(gain_all)
        for g in range(N_E):
            gain_all[g, :, :COLS] = gain[:, g * COLS : (g + 1) * COLS]
        ow_wide[...] = jnp.zeros_like(ow_wide)
        ow_wide[:COLS] = ow[...]

    def ctx_wait():
        for half in (0, 1):
            for d in (1, 3):
                relay_copy(half, d).wait_recv()

    def projected(group):
        total = jnp.zeros((GROUP, WIDE), jnp.float32)
        for half in (0, 1):
            values = ctx_all[half, group].reshape(GROUP, width)
            weight = ow_wide[:, half * width : (half + 1) * width]
            total = total + lax.dot_general(
                values, weight, (((1,), (1,)), ((), ())), preferred_element_type=jnp.float32
            )
        return total

    def part_copy(j):
        return pltpu.make_async_remote_copy(
            part_send.at[j], part_recv.at[j], s_part.at[j], r_part.at[j],
            device_id=(e, (t + j) % N_T), device_id_type=MESH,
        )

    def project():
        for j in (2, 3, 1):
            part_send[j] = projected((t + j) % N_T).astype(jnp.bfloat16)
            part_copy(j).start()
        part_own[...] = projected(t)

    def residual():
        for q in range(8):
            @pl.when(t * 8 + q != e)
            def _(q=q):
                pltpu.make_async_copy(hid_recv.at[q], hid_recv.at[q], r_hid.at[q]).wait()

        resid = part_own[...] + hid_recv[...].reshape(GROUP, WIDE).astype(jnp.float32)
        for j in (1, 2, 3):
            part_copy(j).wait_recv()
            resid = resid + part_recv[j].astype(jnp.float32)
        high, low = split_sum(jnp.sum(resid * resid, axis=1, keepdims=True))
        lane = lax.broadcasted_iota(jnp.int32, (GROUP, WIDE), 1)
        scaled = resid * gain_all[e]
        scaled = jnp.where(lane == COLS, high, jnp.where(lane == COLS + 1, low, scaled))
        msg[y] = scaled.astype(jnp.bfloat16)

    spot_in = (x % 2) * 2 + z

    def lift_copy(d):
        return pltpu.make_async_remote_copy(
            msg.at[y], msg.at[y], s_lift.at[d], r_lift.at[d], device_id=(at(d, 0, 0), t), device_id_type=MESH
        )

    def msg_copy(column):
        target = y * 8 + column * 2 + x // 2
        return target, pltpu.make_async_remote_copy(
            msg.at[column], held.at[t, spot_in], s_msg.at[column], r_msg.at[spot_in],
            device_id=(target, t), device_id_type=MESH,
        )

    def msg_pass(column):
        target, copy = msg_copy(column)

        @pl.when(target != e)
        def _():
            copy.start()

        @pl.when(target == e)
        def _():
            held[t, spot_in] = msg[column]

    def msg_start():
        for d in (2, 1, 3):
            lift_copy(d).start()
        msg_pass(y)

    def msg_on():
        for d in (1, 3, 2):
            source = (y + 4 - d) % 4
            pltpu.make_async_copy(msg.at[source], msg.at[source], r_lift.at[d]).wait()
            msg_pass(source)

    def msg_wait():
        for j in range(4):
            @pl.when((x != 2 * z + j // 2) | (z != j % 2))
            def _(j=j):
                pltpu.make_async_copy(held.at[t, j], held.at[t, j], r_msg.at[j]).wait()

    other_core = t + 1 - 2 * (t % 2)
    other_chip = (t + 2) % N_T
    far = (other_core + 2) % N_T

    def held_copy(i):
        group, target = ((t, other_chip), (t, other_core), (other_chip, other_core))[i]
        return pltpu.make_async_remote_copy(
            held.at[group], held.at[group], s_held.at[i], r_held.at[i], device_id=(e, target), device_id_type=MESH
        )

    def held_start():
        held_copy(0).start()
        held_copy(1).start()

    def held_on():
        held_copy(0).wait_recv()
        held_copy(2).start()

    def pair_copy(group):
        return pltpu.make_async_remote_copy(
            pre_send.at[pl.ds(group * 4, 4), 1 - z], pair_recv.at[pl.ds(group * 4, 4)],
            s_pair.at[group], r_pair.at[group], device_id=(at(0, 0, 1), t), device_id_type=MESH,
        )

    plane_spot = y * 4 + x

    def pre_copy(o):
        return pltpu.make_async_remote_copy(
            pair_sum.at[o], pre_out.at[plane_spot], s_pre.at[o], r_pre.at[plane_spot],
            device_id=(o * 2 + z, t), device_id_type=MESH,
        )

    own_copy = pltpu.make_async_copy(pair_sum.at[plane_spot], pre_out.at[plane_spot], local_sem.at[0])

    def expert_rows(i):
        group = (t, other_core, other_chip, far)[i]
        if i in (1, 3):
            pltpu.make_async_copy(held.at[group], held.at[group], r_held.at[1 if i == 1 else 2]).wait()
        weight = cast[...].reshape(-1, FCOL)
        total = jnp.zeros((GROUP, FCOL), jnp.float32)
        for j in range(4):
            total = total + jnp.dot(
                held[group, j][:, :COLS], weight[j * COLS : (j + 1) * COLS], preferred_element_type=jnp.float32
            )
        pre_send[pl.ds(group * 4, 4)] = total.astype(jnp.bfloat16).reshape(4, 2, TOK_DEV, FCOL)
        pair_copy(group).start()

    def expert_sums(i):
        group = (t, other_core, other_chip, far)[i]
        pair_copy(group).wait_recv()
        rows = pl.ds(group * 4, 4)
        total = pre_send[rows, z].astype(jnp.float32) + pair_recv[rows].astype(jnp.float32)
        pair_sum[rows] = total.astype(jnp.bfloat16)

        @pl.loop(0, 4)
        def _(q):
            o = group * 4 + q

            @pl.when(o != plane_spot)
            def _():
                pre_copy(o).start()

            @pl.when(o == plane_spot)
            def _():
                own_copy.start()

    def square_copy(q):
        return pltpu.make_async_remote_copy(
            square_send.at[q], square_out.at[spot], s_square.at[q], r_square.at[spot],
            device_id=(y * 8 + q, t), device_id_type=MESH,
        )

    own_squares = pltpu.make_async_copy(square_send.at[spot], square_out.at[spot], local_sem.at[1])

    def squares_start():
        tail_lane = lax.broadcasted_iota(jnp.int32, (GROUP, WIDE - GROUP), 1)
        squares = jnp.zeros((GROUP, 1), jnp.float32)
        for j in range(4):
            tail = held[y, j][:, GROUP:].astype(jnp.float32)
            squares = squares + jnp.sum(jnp.where(tail_lane >= COLS - GROUP, tail, 0.0), axis=1, keepdims=True)
        high, low = split_sum(squares)
        extra = jnp.where(tail_lane == 0, high, jnp.where(tail_lane == 1, low, 0.0))
        square_send[...] = extra.astype(jnp.bfloat16).reshape(square_send.shape)
        for q in range(8):
            @pl.when(q != spot)
            def _(q=q):
                square_copy(q).start()

        own_squares.start()

    def finish_decode():
        own_copy.wait()
        own_squares.wait()
        for q in range(8):
            @pl.when(q != spot)
            def _(q=q):
                pltpu.make_async_copy(square_send.at[q], square_out.at[q], r_square.at[q]).wait()
                square_copy(q).wait_send()

        for group in range(4):
            pair_copy(group).wait_send()

        @pl.loop(1, N_E // 2)
        def _(i):
            source = (plane_spot + i) % (N_E // 2)
            pltpu.make_async_copy(pair_sum.at[source], pre_out.at[source], r_pre.at[source]).wait()
            pre_copy(source).wait_send()

        @pl.when(sends_hidden)
        def _():
            @pl.loop(1, N_E)
            def _(i):
                hid_copy(i).wait_send()

        for half in (0, 1):
            for i in range(1, 8):
                ctx_copy(half, i).wait_send()
            for d in (1, 3):
                row_copy(half, d).wait_send()
                relay_copy(half, d).wait_send()
        for j in (1, 2, 3):
            part_copy(j).wait_send()
            held_copy(j - 1).wait_send()
        for column in range(4):
            target, copy = msg_copy(column)

            @pl.when(target != e)
            def _(copy=copy):
                copy.wait_send()
        for d in (1, 2, 3):
            lift_copy(d).wait_send()

    optimize(0, EARLY)
    barrier_wait()
    ctx_start()
    near_start("z", "own+", "own-")
    optimize(EARLY, blocks - EARLY)
    row_start()
    near_start("z b", "own+ b", "own- b")
    make_table()
    prepare()
    hid_start()
    row_on()
    pick(0, 0)
    pick(1, 0)
    ctx_wait()
    project()
    near_wait(0, "z")
    near_copy(0, "z+").start()
    near_copy(0, "z-").start()
    near_wait(1, "z")
    near_copy(1, "z+").start()
    near_copy(1, "z-").start()
    residual()
    msg_start()
    near_wait(0, "own+")
    near_copy(0, "on+").start()
    near_wait(1, "own+")
    near_copy(1, "on+").start()
    near_wait(2, "own+")
    near_copy(2, "on+").start()
    near_wait(3, "own+")
    near_copy(3, "on+").start()
    near_wait(2, "own-")
    near_copy(2, "on-").start()
    near_wait(3, "own-")
    near_copy(3, "on-").start()
    msg_on()
    pick(2, 0)
    pick(3, 0)
    pick(0, 0, 1)
    pick(1, 0, 1)
    msg_wait()
    held_start()
    pick(2, 1)
    pick(3, 1)
    near_wait(0, "z-")
    near_copy(0, "on-").start()
    near_wait(1, "z-")
    near_copy(1, "on-").start()
    pick(0, 3)
    pick(1, 3)
    held_on()
    near_wait(0, "own-")
    pick(0, 1)
    near_wait(1, "own-")
    pick(1, 1)
    expert_rows(0)
    expert_rows(1)
    expert_rows(2)
    expert_rows(3)
    squares_start()
    pick(0, 1, 1)
    pick(1, 1, 1)
    pick(2, 3)
    expert_sums(0)
    expert_sums(1)
    expert_sums(2)
    expert_sums(3)
    pick(3, 3)
    near_wait(0, "z+")
    pick(0, 3, 1)
    near_wait(1, "z+")
    pick(1, 3, 1)
    near_wait(2, "on+")
    near_wait(2, "on-")
    pick(2, 2)
    near_wait(3, "on+")
    near_wait(3, "on-")
    pick(3, 2)
    near_wait(0, "on+")
    pick(0, 2)
    near_wait(1, "on+")
    pick(1, 2)
    near_wait(0, "on-")
    pick(0, 2, 1)
    near_wait(1, "on-")
    pick(1, 2, 1)
    optimize_end()
    finish_decode()
    rollout_end()


def step(master, grad, first, second, context, out_weight, hidden, norm_gain, plan):
    anywhere = pl.BlockSpec(memory_space=pl.ANY)
    dma = pltpu.SemaphoreType.DMA
    bf16 = jnp.bfloat16
    blocks, block_rows, columns = master.shape
    state = jax.ShapeDtypeStruct(master.shape, jnp.float32)
    depth = out_weight.shape[0]
    width = hidden.shape[1]
    return pl.pallas_call(
        step_kernel,
        out_shape=(
            jax.ShapeDtypeStruct((N_E // 2, TOK_DEV, FCOL), bf16),
            jax.ShapeDtypeStruct((8, TOK_DEV, GROUP), bf16),
            jax.ShapeDtypeStruct((4, 4, 2, CAP, block_rows, columns), bf16),
            state, state, state,
        ),
        in_specs=[anywhere] * 9,
        out_specs=(anywhere,) * 6,
        scratch_shapes=[
            pltpu.SMEM((N_E, 128), jnp.int32),
            pltpu.VMEM(master.shape, bf16),
            pltpu.VMEM((3, *master.shape), jnp.float32),
            pltpu.VMEM(master.shape, bf16),
            pltpu.VMEM((3, *master.shape), jnp.float32),
            pltpu.VMEM((N_E, 128), jnp.int32),
            dma((3 * blocks,)), dma((blocks,)), dma((3 * blocks,)), dma,
            pltpu.VMEM((COLS, depth), bf16),
            pltpu.VMEM((TOK_DEV, width), bf16),
            pltpu.VMEM((1, width), jnp.float32),
            pltpu.VMEM((8, 128), jnp.int32),
            dma((4,)),
            pltpu.VMEM((2, 4, 4, 2, TOK_DEV, depth // 2), bf16),
            pltpu.VMEM((WIDE, depth), bf16),
            pltpu.VMEM((N_E, TOK_DEV, WIDE), bf16),
            pltpu.VMEM((8, TOK_DEV, WIDE), bf16),
            pltpu.VMEM((N_E, 1, WIDE), jnp.float32),
            pltpu.VMEM((N_T, GROUP, WIDE), bf16),
            pltpu.VMEM((N_T, GROUP, WIDE), bf16),
            pltpu.VMEM((GROUP, WIDE), jnp.float32),
            pltpu.VMEM((4, GROUP, WIDE), bf16),
            pltpu.VMEM((N_T, 4, GROUP, WIDE), bf16),
            pltpu.VMEM((N_E // 2, 2, TOK_DEV, FCOL), bf16),
            pltpu.VMEM((N_E // 2, TOK_DEV, FCOL), bf16),
            pltpu.VMEM((N_E // 2, TOK_DEV, FCOL), bf16),
            dma((4,)), dma((4,)),
            dma((16,)), dma((16,)), dma((8,)), dma((8,)),
            dma((N_E,)), dma((8,)), dma((N_T,)), dma((N_T,)), dma((4,)), dma((4,)), dma((4,)), dma((4,)),
            dma((3,)), dma((3,)), dma((N_E // 2,)), dma((N_E // 2,)), dma((2,)),
            pltpu.VMEM((8, TOK_DEV, GROUP), bf16), dma((8,)), dma((8,)),
            dma((40,)), dma((40,)), dma((128,)), dma((128,)),
            *[pltpu.VMEM((32, CAP, rows, columns), bf16) for _, _, _, rows in PARTS],
            *[
                pltpu.VMEM((blocks, rows, columns), bf16)
                for _, z_first, _, rows in PARTS
                for _ in range(7 if z_first else 3)
            ],
        ],
        compiler_params=pltpu.CompilerParams(
            collective_id=0, has_side_effects=True, vmem_limit_bytes=56 * 2**20
        ),
        name="step",
    )(
        master, grad, first, second, context, out_weight.T, hidden, norm_gain.reshape(1, -1), plan.reshape(8, 128)
    )


def finish_kernel(
    plan_in, route_in, partial_in, squares_in, roll, master_in, first_in, second_in,
    out, rollout, master, first, second,
    plan, route, stage, state, partial, square_parts, seen, in_sems, out_sems, state_in_sems, state_out_sems, decode_sems,
):
    e = lax.axis_index("expert")
    slots = rollout.shape[0]
    sources, targets = (master_in, first_in, second_in), (master, first, second)

    def fetch(j, place):
        return pltpu.make_async_copy(roll.at[place], stage.at[j], in_sems.at[j])

    def store(j):
        return pltpu.make_async_copy(stage.at[j], rollout.at[j], out_sems.at[j])

    def state_in(i):
        return pltpu.make_async_copy(sources[i], state.at[i], state_in_sems.at[i])

    def state_out(i):
        return pltpu.make_async_copy(state.at[i], targets[i], state_out_sems.at[i])

    partial_copy = pltpu.make_async_copy(partial_in, partial, decode_sems.at[0])
    squares_copy = pltpu.make_async_copy(squares_in, square_parts, decode_sems.at[1])
    plan_copy = pltpu.make_async_copy(plan_in, plan, decode_sems.at[2])
    route_copy = pltpu.make_async_copy(route_in, route, decode_sems.at[3])
    plan_copy.start()
    route_copy.start()
    for i in range(3):
        state_in(i).start()

    @pl.loop(0, N_E)
    def _(j):
        seen[j] = 0

    plan_copy.wait()
    route_copy.wait()

    @pl.loop(0, slots)
    def _(j):
        source = (plan[e * slots + j] * 9363) >> 16
        rank = seen[source]
        seen[source] = rank + 1
        dy = (source // 8 + 4 - e // 8) % 4
        dx = (source // 2 + 4 - (e // 2) % 4) % 4
        dz = (source + e) % 2
        fetch(j, ((dx * 4 + dy) * 2 + dz) * CAP + rank).start()

    partial_copy.start()
    squares_copy.start()
    for i in range(3):
        state_in(i).wait()
        state_out(i).start()

    @pl.loop(0, slots)
    def _(j):
        fetch(j, 0).wait()
        store(j).start()

    partial_copy.wait()
    squares_copy.wait()
    token = lax.broadcasted_iota(jnp.int32, (TOK_DEV, 1), 0)
    expert = jnp.zeros((TOK_DEV, 1), jnp.int32)
    for i in range(TOK_DEV):
        expert = jnp.where(token == i, route[e * TOK_DEV + i], expert)
    pre = jnp.zeros((TOK_DEV, FCOL), jnp.float32)
    squares = jnp.zeros((TOK_DEV, 1), jnp.float32)
    for k in range(4):
        total = jnp.zeros((TOK_DEV, FCOL), jnp.float32)
        for h in range(4):
            total = total + partial[k * 4 + h].astype(jnp.float32)
        pre = pre + jnp.where(expert == k, total, 0.0)
    for h in range(8):
        squares = squares + jnp.sum(square_parts[h].astype(jnp.float32), axis=1, keepdims=True)
    pre = pre * lax.rsqrt(squares / (N_E * COLS) + 1e-06)
    out[...] = (pre / (1.0 + jnp.exp(-pre))).astype(jnp.bfloat16)

    @pl.loop(0, slots)
    def _(j):
        store(j).wait()

    for i in range(3):
        state_out(i).wait()


def finish(plan, route, partial, squares, roll, state):
    vmem = pl.BlockSpec(memory_space=pltpu.VMEM)
    anywhere = pl.BlockSpec(memory_space=pl.ANY)
    block_rows, columns = roll.shape[-2:]
    slots = plan.shape[0] // N_E
    shape = jax.ShapeDtypeStruct(state[0].shape, jnp.float32)
    dma = pltpu.SemaphoreType.DMA
    return pl.pallas_call(
        finish_kernel,
        out_shape=(
            jax.ShapeDtypeStruct((TOK_DEV, FCOL), jnp.bfloat16),
            jax.ShapeDtypeStruct((slots, block_rows, columns), jnp.bfloat16),
            shape, shape, shape,
        ),
        in_specs=[anywhere] * 8,
        out_specs=(vmem,) + (anywhere,) * 4,
        scratch_shapes=[
            pltpu.SMEM(plan.shape, jnp.int32),
            pltpu.SMEM(route.shape, jnp.int32),
            pltpu.VMEM((slots, block_rows, columns), jnp.bfloat16),
            pltpu.VMEM((3, *state[0].shape), jnp.float32),
            pltpu.VMEM(partial.shape, partial.dtype),
            pltpu.VMEM(squares.shape, squares.dtype),
            pltpu.SMEM((N_E,), jnp.int32),
            dma((slots,)), dma((slots,)), dma((3,)), dma((3,)), dma((4,)),
        ],
        compiler_params=pltpu.CompilerParams(vmem_limit_bytes=56 * 2**20),
        name="finish",
    )(plan, route, partial, squares, roll.reshape(4 * 4 * 2 * CAP, block_rows, columns), *state)


def shards(
    master, grad, moment_one, moment_two, context, out_weight, hidden, norm_gain, route, plan
):
    partial, squares, roll, *state = step(
        master, grad, moment_one, moment_two, context, out_weight, hidden, norm_gain, plan
    )
    activation, rollout, *state = finish(plan, route, partial, squares, roll, state)
    return (*state, rollout, activation)


def solution(mesh):
    return jax.shard_map(
        shards,
        mesh=mesh,
        in_specs=(
            P("expert", None, "tensor"),
            P("expert", None, "tensor"),
            P("expert", None, "tensor"),
            P("expert", None, "tensor"),
            P("expert", "tensor"),
            P("tensor", "expert"),
            P("expert", None),
            P(),
            P(),
            P(),
        ),
        out_specs=(
            P("expert", None, "tensor"),
            P("expert", None, "tensor"),
            P("expert", None, "tensor"),
            P("expert", None, "tensor"),
            P("expert", "tensor"),
        ),
        check_vma=False,
    )
```

```python
import functools

import jax
import jax.numpy as jnp
from jax import lax
from jax.experimental import pallas as pl
from jax.experimental.pallas import tpu as pltpu
from jax.sharding import PartitionSpec as P

MESH = pl.DeviceIdType.MESH
CAP = 2
N_E = 32
N_T = 4
TOK_DEV = 16
COLS = 224
WIDE = 256
GROUP = 128
FCOL = 512
HALF = 64

beta_one = 0.9
beta_two = 0.95
bias_one = 1.0 - 0.9**50
bias_two = 1.0 - 0.95**50
learn_rate = 0.0003
decay_rate = 0.1
adam_eps = 1e-08


def split_sum(total):
    high = total.astype(jnp.bfloat16)
    low = (total - high.astype(jnp.float32)).astype(jnp.bfloat16)
    return high.astype(jnp.float32), low.astype(jnp.float32)


def parts_of(wide, narrow):
    parts = [(0, True, 0, wide), (1, True, wide, wide)]
    if narrow:
        parts += [(0, False, 2 * wide, narrow), (1, False, 2 * wide + narrow, narrow)]
    return parts


PARTS = parts_of(48, 16)
EARLY = 2


def step_kernel(
    master, grad, first, second, ctx, ow_in, hid_in, gain_in, plan_in,
    pre_out, square_out, roll, new_master, new_first, new_second,
    table, cast, state_in, grad_in, state_out, sent_index, s_state, s_grad, s_out, s_table,
    ow, hid, gain, plan, s_load, ctx_all,
    ow_wide, hid_send, hid_recv, gain_all, part_send, part_recv, part_own, msg, held, pre_send, pair_recv, pair_sum, s_pair, r_pair,
    s_ctx, r_ctx, s_row, r_row, s_hid, r_hid, s_part, r_part, s_lift, r_lift, s_msg, r_msg, s_held, r_held, s_pre, r_pre, local_sem,
    square_send, s_square, r_square, s_near, r_near, s_pick, r_pick, *rest
):
    picked = rest[: len(PARTS)]
    near = []
    used = len(PARTS)
    for _, z_first, _, _ in PARTS:
        count = 7 if z_first else 3
        near.append(rest[used : used + count])
        used += count
    e = lax.axis_index("expert")
    t = lax.axis_index("tensor")
    y, x, z = e // 8, (e // 2) % 4, e % 2

    barrier = pltpu.get_barrier_semaphore()

    @pl.loop(1, N_E)
    def _(i):
        pl.semaphore_signal(barrier, 1, device_id=((e + i) % N_E, t), device_id_type=MESH)

    for j in range(1, N_T):
        pl.semaphore_signal(barrier, 1, device_id=(e, (t + j) % N_T), device_id_type=MESH)

    loads = [
        pltpu.make_async_copy(source, target, s_load.at[i])
        for i, (source, target) in enumerate(((ow_in, ow), (hid_in, hid), (gain_in, gain), (plan_in, plan)))
    ]
    for load in loads:
        load.start()

    blocks = cast.shape[0]
    arrays_in, arrays_out = (master, first, second), (new_master, new_first, new_second)

    def state_copy(b, i):
        return pltpu.make_async_copy(arrays_in[i].at[b], state_in.at[i, b], s_state.at[b * 3 + i])

    def grad_copy(b):
        return pltpu.make_async_copy(grad.at[b], grad_in.at[b], s_grad.at[b])

    @pl.loop(0, blocks)
    def _(b):
        for i in range(3):
            state_copy(b, i).start()
        grad_copy(b).start()

    def barrier_wait():
        pl.semaphore_wait(barrier, N_E - 1 + N_T - 1)

    def at(dy, dx, dz):
        return ((y + dy) % 4) * 8 + ((x + dx) % 4) * 2 + (z + dz) % 2

    def gather_to(axis, d, dz=0):
        return at(d, 0, dz) if axis == 0 else at(0, d, dz)

    def owner_at(axis, d, dz=0):
        return at(0, d, dz) if axis == 0 else at(d, 0, dz)

    def place_of(p, d, dz):
        return 2 * d + dz if PARTS[p][1] else d

    FIRST, SECOND = (0, 4), (4, 3)
    HEAD, TAIL = (0, EARLY), (EARLY, blocks - EARLY)

    def step_of(p, step):
        if PARTS[p][1]:
            return {
                "z": (None, 1, 0, 1, HEAD),
                "own+": (None, 6, 1, 0, HEAD),
                "own-": (None, 2, 3, 0, HEAD),
                "z b": (None, 1, 0, 1, TAIL),
                "own+ b": (None, 6, 1, 0, TAIL),
                "own- b": (None, 2, 3, 0, TAIL),
                "z+": (1, 7, 1, 0, None),
                "z-": (1, 3, 3, 0, None),
                "on+": (6, 4, 1, 0, None),
                "on-": (3, 5, 3, 0, None),
            }[step]
        return {
            "own+": (None, 3, 1, 0, HEAD),
            "own-": (None, 1, 3, 0, HEAD),
            "own+ b": (None, 3, 1, 0, TAIL),
            "own- b": (None, 1, 3, 0, TAIL),
            "on+": (3, 2, 1, 0, FIRST),
            "on-": (1, 2, 3, 0, SECOND),
        }[step]

    def steps_of(p):
        shared = ("own+", "own-", "own+ b", "own- b", "on+", "on-")
        return (*shared, "z", "z b", "z+", "z-") if PARTS[p][1] else shared

    def near_copy(p, step):
        axis, _, row, rows = PARTS[p]
        source, place, d, dz, some = step_of(p, step)
        index = p * 10 + steps_of(p).index(step)
        some = pl.ds(*(some or (0, blocks)))
        piece = cast.at[some, pl.ds(row, rows)] if source is None else near[p][source - 1].at[some]
        target = near[p][place - 1].at[some]
        return pltpu.make_async_remote_copy(
            piece, target, s_near.at[index], r_near.at[index],
            device_id=(gather_to(axis, d, dz), t), device_id_type=MESH,
        )

    def near_start(*steps):
        for p in range(len(PARTS)):
            for step in steps:
                if step in steps_of(p):
                    near_copy(p, step).start()

    def near_wait(p, step):
        near_copy(p, step).wait_recv()
        if step + " b" in steps_of(p):
            near_copy(p, step + " b").wait_recv()

    def targets(p):
        return [(d, dz) for dz in ((0,) if PARTS[p][1] else (1, 0)) for d in (1, 3, 2, 0)]

    def pick_copy(p, d, dz, od, odz):
        axis, z_first, row, rows = PARTS[p]
        place = place_of(p, d, dz)
        index = p * 32 + place * len(targets(p)) + targets(p).index((od, odz))
        back = (4 - od) % 4
        slot = roll.at[(back, d, dz + odz) if axis == 0 else (d, back, dz + odz)]
        source, target = picked[p].at[index - p * 32], slot.at[:, pl.ds(row, rows)]
        if (od, odz) == (0, 0):
            return pltpu.make_async_copy(source, target, s_pick.at[index])
        return pltpu.make_async_remote_copy(
            source, target, s_pick.at[index], r_pick.at[index],
            device_id=(owner_at(axis, od, odz), t), device_id_type=MESH,
        )

    def pick(p, d, dz=0):
        axis, _, row, rows = PARTS[p]
        place = place_of(p, d, dz)
        source = gather_to(axis, d, dz)
        for i, (od, odz) in enumerate(targets(p)):
            owner = owner_at(axis, od, odz)
            for r in range(CAP):
                block = table[(owner % 4) * 8 + owner // 4, source * CAP + r]
                if place == 0:
                    found = cast[block, pl.ds(row, rows)]
                else:
                    found = near[p][place - 1][block]
                picked[p][place * len(targets(p)) + i, r] = found
            pick_copy(p, d, dz, od, odz).start()

    def rollout_end():
        for p in range(len(PARTS)):
            for step in steps_of(p):
                near_copy(p, step).wait_send()
        for d, dz in ((0, 0), (0, 1), (1, 0), (3, 0), (1, 1), (3, 1), (2, 0), (2, 1)):
            for p in range(len(PARTS)):
                if PARTS[p][1] or dz == 0:
                    for od, odz in targets(p):
                        pick_copy(p, d, dz, od, odz).wait()

    def out_copy(b, i):
        return pltpu.make_async_copy(state_out.at[i, b], arrays_out[i].at[b], s_out.at[b * 3 + i])

    def optimize(start, count):
        @pl.loop(start, start + count)
        def _(b):
            for i in range(3):
                state_copy(b, i).wait()
            grad_copy(b).wait()

            @pl.loop(0, cast.shape[1] // 32)
            def _(row):
                rows = pl.ds(pl.multiple_of(row * 32, 32), 32)
                weight = state_in[0, b, rows]
                gradient = grad_in[b, rows].astype(jnp.float32)
                one = beta_one * state_in[1, b, rows] + (1.0 - beta_one) * gradient
                two = beta_two * state_in[2, b, rows] + (1.0 - beta_two) * gradient * gradient
                update = (one * (1.0 / bias_one)) / (jnp.sqrt(two * (1.0 / bias_two)) + adam_eps) + decay_rate * weight
                weight = weight - learn_rate * update
                state_out[0, b, rows] = weight
                state_out[1, b, rows] = one
                state_out[2, b, rows] = two
                cast[b, rows] = weight.astype(jnp.bfloat16)

            for i in range(3):
                out_copy(b, i).start()

    def optimize_end():
        @pl.loop(0, blocks)
        def _(b):
            for i in range(3):
                out_copy(b, i).wait()

    table_copy = pltpu.make_async_copy(sent_index, table, s_table)

    def make_table():
        loads[3].wait()
        wanted = plan[...]
        source = (wanted * 9363) >> 16
        local = wanted - source * blocks
        lane = lax.broadcasted_iota(jnp.int32, wanted.shape, 1)
        slot = lane % N_E
        rank = jnp.zeros_like(wanted)
        for j in range(1, N_E):
            rank = rank + jnp.where((pltpu.roll(source, j, 1) == source) & (slot >= j), 1, 0)
        key = source * CAP + rank
        for quarter in range(4):
            found = jnp.zeros_like(wanted)
            for j in range(N_E):
                at_lane = quarter * N_E + j
                found = found + jnp.where(key[:, at_lane : at_lane + 1] == lane, local[:, at_lane : at_lane + 1], 0)
            sent_index[pl.ds(quarter * 8, 8)] = found
        table_copy.start()
        table_copy.wait()

    width = ctx_all.shape[-1]

    def ctx_copy(half, i):
        target = gather_to(half, i // 2, i % 2)
        return pltpu.make_async_remote_copy(
            ctx.at[:, pl.ds(half * width, width)], ctx_all.at[half, y, x, z], s_ctx.at[half * 8 + i], r_ctx.at[half * 8 + i],
            device_id=(target, t), device_id_type=MESH,
        )

    def row_copy(half, d):
        rows = ctx_all.at[0, :, x] if half == 0 else ctx_all.at[1, y]
        return pltpu.make_async_remote_copy(
            rows, rows, s_row.at[half * 4 + d], r_row.at[half * 4 + d],
            device_id=(owner_at(half, d), t), device_id_type=MESH,
        )

    def relay_copy(half, d):
        some = pl.ds(0 if d == 1 else 2, 2)
        rows = ctx_all.at[0, some, (x + 4 - d) % 4] if half == 0 else ctx_all.at[1, (y + 4 - d) % 4, some]
        index = half * 4 + d - 1
        return pltpu.make_async_remote_copy(
            rows, rows, s_row.at[index], r_row.at[index],
            device_id=(owner_at(half, d), t), device_id_type=MESH,
        )

    def ctx_own(half):
        return pltpu.make_async_copy(
            ctx.at[:, pl.ds(half * width, width)], ctx_all.at[half, y, x, z], s_ctx.at[half * 8]
        )

    def ctx_start():
        for half in (0, 1):
            for i in range(1, 8):
                ctx_copy(half, i).start()
            ctx_own(half).start()

    def row_start():
        for half in (0, 1):
            ctx_own(half).wait()
            for i in range(1, 8):
                ctx_copy(half, i).wait_recv()
            for d in (1, 3):
                row_copy(half, d).start()

    def row_on():
        for half in (0, 1):
            for d in (1, 3):
                row_copy(half, d).wait_recv()
                relay_copy(half, d).start()

    spot = x * 2 + z
    sends_hidden = y == t

    def hid_copy(i):
        return pltpu.make_async_remote_copy(
            hid_send.at[(e + i) % N_E], hid_recv.at[spot], s_hid.at[i], r_hid.at[spot],
            device_id=((e + i) % N_E, t), device_id_type=MESH,
        )

    def hid_start():
        loads[1].wait()

        @pl.when(sends_hidden)
        def _():
            hid_send[...] = jnp.zeros_like(hid_send)
            for g in range(N_E):
                hid_send[g, :, :COLS] = hid[:, g * COLS : (g + 1) * COLS]

            @pl.loop(1, N_E)
            def _(i):
                hid_copy(i).start()

            hid_recv[spot] = hid_send[e]

    def prepare():
        loads[0].wait()
        loads[2].wait()
        gain_all[...] = jnp.zeros_like(gain_all)
        for g in range(N_E):
            gain_all[g, :, :COLS] = gain[:, g * COLS : (g + 1) * COLS]
        ow_wide[...] = jnp.zeros_like(ow_wide)
        ow_wide[:COLS] = ow[...]

    def ctx_wait():
        for half in (0, 1):
            for d in (1, 3):
                relay_copy(half, d).wait_recv()

    def projected(group):
        total = jnp.zeros((GROUP, WIDE), jnp.float32)
        for half in (0, 1):
            values = ctx_all[half, group].reshape(GROUP, width)
            weight = ow_wide[:, half * width : (half + 1) * width]
            total = total + lax.dot_general(
                values, weight, (((1,), (1,)), ((), ())), preferred_element_type=jnp.float32
            )
        return total

    def part_copy(j):
        return pltpu.make_async_remote_copy(
            part_send.at[j], part_recv.at[j], s_part.at[j], r_part.at[j],
            device_id=(e, (t + j) % N_T), device_id_type=MESH,
        )

    def project():
        for j in (2, 3, 1):
            part_send[j] = projected((t + j) % N_T).astype(jnp.bfloat16)
            part_copy(j).start()
        part_own[...] = projected(t)

    def residual():
        for q in range(8):
            @pl.when(t * 8 + q != e)
            def _(q=q):
                pltpu.make_async_copy(hid_recv.at[q], hid_recv.at[q], r_hid.at[q]).wait()

        resid = part_own[...] + hid_recv[...].reshape(GROUP, WIDE).astype(jnp.float32)
        for j in (1, 2, 3):
            part_copy(j).wait_recv()
            resid = resid + part_recv[j].astype(jnp.float32)
        high, low = split_sum(jnp.sum(resid * resid, axis=1, keepdims=True))
        lane = lax.broadcasted_iota(jnp.int32, (GROUP, WIDE), 1)
        scaled = resid * gain_all[e]
        scaled = jnp.where(lane == COLS, high, jnp.where(lane == COLS + 1, low, scaled))
        msg[y] = scaled.astype(jnp.bfloat16)

    spot_in = (x % 2) * 2 + z

    def lift_copy(d):
        return pltpu.make_async_remote_copy(
            msg.at[y], msg.at[y], s_lift.at[d], r_lift.at[d], device_id=(at(d, 0, 0), t), device_id_type=MESH
        )

    def msg_copy(column):
        target = y * 8 + column * 2 + x // 2
        return target, pltpu.make_async_remote_copy(
            msg.at[column], held.at[t, spot_in], s_msg.at[column], r_msg.at[spot_in],
            device_id=(target, t), device_id_type=MESH,
        )

    def msg_pass(column):
        target, copy = msg_copy(column)

        @pl.when(target != e)
        def _():
            copy.start()

        @pl.when(target == e)
        def _():
            held[t, spot_in] = msg[column]

    def msg_start():
        for d in (2, 1, 3):
            lift_copy(d).start()
        msg_pass(y)

    def msg_on():
        for d in (1, 3, 2):
            source = (y + 4 - d) % 4
            pltpu.make_async_copy(msg.at[source], msg.at[source], r_lift.at[d]).wait()
            msg_pass(source)

    def msg_wait():
        for j in range(4):
            @pl.when((x != 2 * z + j // 2) | (z != j % 2))
            def _(j=j):
                pltpu.make_async_copy(held.at[t, j], held.at[t, j], r_msg.at[j]).wait()

    other_core = t + 1 - 2 * (t % 2)
    other_chip = (t + 2) % N_T
    far = (other_core + 2) % N_T

    def held_copy(i):
        group, target = ((t, other_chip), (t, other_core), (other_chip, other_core))[i]
        return pltpu.make_async_remote_copy(
            held.at[group], held.at[group], s_held.at[i], r_held.at[i], device_id=(e, target), device_id_type=MESH
        )

    def held_start():
        held_copy(0).start()
        held_copy(1).start()

    def held_on():
        held_copy(0).wait_recv()
        held_copy(2).start()

    def pair_copy(group):
        return pltpu.make_async_remote_copy(
            pre_send.at[pl.ds(group * 4, 4), 1 - z], pair_recv.at[pl.ds(group * 4, 4)],
            s_pair.at[group], r_pair.at[group], device_id=(at(0, 0, 1), t), device_id_type=MESH,
        )

    plane_spot = y * 4 + x

    def pre_copy(o):
        return pltpu.make_async_remote_copy(
            pair_sum.at[o], pre_out.at[plane_spot], s_pre.at[o], r_pre.at[plane_spot],
            device_id=(o * 2 + z, t), device_id_type=MESH,
        )

    own_copy = pltpu.make_async_copy(pair_sum.at[plane_spot], pre_out.at[plane_spot], local_sem.at[0])

    def expert_rows(i):
        group = (t, other_core, other_chip, far)[i]
        if i in (1, 3):
            pltpu.make_async_copy(held.at[group], held.at[group], r_held.at[1 if i == 1 else 2]).wait()
        weight = cast[...].reshape(-1, FCOL)
        total = jnp.zeros((GROUP, FCOL), jnp.float32)
        for j in range(4):
            total = total + jnp.dot(
                held[group, j][:, :COLS], weight[j * COLS : (j + 1) * COLS], preferred_element_type=jnp.float32
            )
        pre_send[pl.ds(group * 4, 4)] = total.astype(jnp.bfloat16).reshape(4, 2, TOK_DEV, FCOL)
        pair_copy(group).start()

    def expert_sums(i):
        group = (t, other_core, other_chip, far)[i]
        pair_copy(group).wait_recv()
        rows = pl.ds(group * 4, 4)
        total = pre_send[rows, z].astype(jnp.float32) + pair_recv[rows].astype(jnp.float32)
        pair_sum[rows] = total.astype(jnp.bfloat16)

        @pl.loop(0, 4)
        def _(q):
            o = group * 4 + q

            @pl.when(o != plane_spot)
            def _():
                pre_copy(o).start()

            @pl.when(o == plane_spot)
            def _():
                own_copy.start()

    def square_copy(q):
        return pltpu.make_async_remote_copy(
            square_send.at[q], square_out.at[spot], s_square.at[q], r_square.at[spot],
            device_id=(y * 8 + q, t), device_id_type=MESH,
        )

    own_squares = pltpu.make_async_copy(square_send.at[spot], square_out.at[spot], local_sem.at[1])

    def squares_start():
        tail_lane = lax.broadcasted_iota(jnp.int32, (GROUP, WIDE - GROUP), 1)
        squares = jnp.zeros((GROUP, 1), jnp.float32)
        for j in range(4):
            tail = held[y, j][:, GROUP:].astype(jnp.float32)
            squares = squares + jnp.sum(jnp.where(tail_lane >= COLS - GROUP, tail, 0.0), axis=1, keepdims=True)
        high, low = split_sum(squares)
        extra = jnp.where(tail_lane == 0, high, jnp.where(tail_lane == 1, low, 0.0))
        square_send[...] = extra.astype(jnp.bfloat16).reshape(square_send.shape)
        for q in range(8):
            @pl.when(q != spot)
            def _(q=q):
                square_copy(q).start()

        own_squares.start()

    def finish_decode():
        own_copy.wait()
        own_squares.wait()
        for q in range(8):
            @pl.when(q != spot)
            def _(q=q):
                pltpu.make_async_copy(square_send.at[q], square_out.at[q], r_square.at[q]).wait()
                square_copy(q).wait_send()

        for group in range(4):
            pair_copy(group).wait_send()

        @pl.loop(1, N_E // 2)
        def _(i):
            source = (plane_spot + i) % (N_E // 2)
            pltpu.make_async_copy(pair_sum.at[source], pre_out.at[source], r_pre.at[source]).wait()
            pre_copy(source).wait_send()

        @pl.when(sends_hidden)
        def _():
            @pl.loop(1, N_E)
            def _(i):
                hid_copy(i).wait_send()

        for half in (0, 1):
            for i in range(1, 8):
                ctx_copy(half, i).wait_send()
            for d in (1, 3):
                row_copy(half, d).wait_send()
                relay_copy(half, d).wait_send()
        for j in (1, 2, 3):
            part_copy(j).wait_send()
            held_copy(j - 1).wait_send()
        for column in range(4):
            target, copy = msg_copy(column)

            @pl.when(target != e)
            def _(copy=copy):
                copy.wait_send()
        for d in (1, 2, 3):
            lift_copy(d).wait_send()

    optimize(0, EARLY)
    barrier_wait()
    ctx_start()
    near_start("z", "own+", "own-")
    optimize(EARLY, blocks - EARLY)
    row_start()
    near_start("z b", "own+ b", "own- b")
    make_table()
    prepare()
    hid_start()
    row_on()
    pick(0, 0)
    pick(1, 0)
    ctx_wait()
    project()
    near_wait(0, "z")
    near_copy(0, "z+").start()
    near_copy(0, "z-").start()
    near_wait(1, "z")
    near_copy(1, "z+").start()
    near_copy(1, "z-").start()
    residual()
    msg_start()
    near_wait(0, "own+")
    near_copy(0, "on+").start()
    near_wait(1, "own+")
    near_copy(1, "on+").start()
    near_wait(2, "own+")
    near_copy(2, "on+").start()
    near_wait(3, "own+")
    near_copy(3, "on+").start()
    near_wait(2, "own-")
    near_copy(2, "on-").start()
    near_wait(3, "own-")
    near_copy(3, "on-").start()
    msg_on()
    pick(2, 0)
    pick(3, 0)
    pick(0, 0, 1)
    pick(1, 0, 1)
    msg_wait()
    held_start()
    pick(2, 1)
    pick(3, 1)
    near_wait(0, "z-")
    near_copy(0, "on-").start()
    near_wait(1, "z-")
    near_copy(1, "on-").start()
    pick(0, 3)
    pick(1, 3)
    held_on()
    near_wait(0, "own-")
    pick(0, 1)
    near_wait(1, "own-")
    pick(1, 1)
    expert_rows(0)
    expert_rows(1)
    expert_rows(2)
    expert_rows(3)
    squares_start()
    pick(0, 1, 1)
    pick(1, 1, 1)
    pick(2, 3)
    expert_sums(0)
    expert_sums(1)
    expert_sums(2)
    expert_sums(3)
    pick(3, 3)
    near_wait(0, "z+")
    pick(0, 3, 1)
    near_wait(1, "z+")
    pick(1, 3, 1)
    near_wait(2, "on+")
    near_wait(2, "on-")
    pick(2, 2)
    near_wait(3, "on+")
    near_wait(3, "on-")
    pick(3, 2)
    near_wait(0, "on+")
    pick(0, 2)
    near_wait(1, "on+")
    pick(1, 2)
    near_wait(0, "on-")
    pick(0, 2, 1)
    near_wait(1, "on-")
    pick(1, 2, 1)
    optimize_end()
    finish_decode()
    rollout_end()


def step(master, grad, first, second, context, out_weight, hidden, norm_gain, plan):
    anywhere = pl.BlockSpec(memory_space=pl.ANY)
    dma = pltpu.SemaphoreType.DMA
    bf16 = jnp.bfloat16
    blocks, block_rows, columns = master.shape
    state = jax.ShapeDtypeStruct(master.shape, jnp.float32)
    depth = out_weight.shape[0]
    width = hidden.shape[1]
    return pl.pallas_call(
        step_kernel,
        out_shape=(
            jax.ShapeDtypeStruct((N_E // 2, TOK_DEV, FCOL), bf16),
            jax.ShapeDtypeStruct((8, TOK_DEV, GROUP), bf16),
            jax.ShapeDtypeStruct((4, 4, 2, CAP, block_rows, columns), bf16),
            state, state, state,
        ),
        in_specs=[anywhere] * 9,
        out_specs=(anywhere,) * 6,
        scratch_shapes=[
            pltpu.SMEM((N_E, 128), jnp.int32),
            pltpu.VMEM(master.shape, bf16),
            pltpu.VMEM((3, *master.shape), jnp.float32),
            pltpu.VMEM(master.shape, bf16),
            pltpu.VMEM((3, *master.shape), jnp.float32),
            pltpu.VMEM((N_E, 128), jnp.int32),
            dma((3 * blocks,)), dma((blocks,)), dma((3 * blocks,)), dma,
            pltpu.VMEM((COLS, depth), bf16),
            pltpu.VMEM((TOK_DEV, width), bf16),
            pltpu.VMEM((1, width), jnp.float32),
            pltpu.VMEM((8, 128), jnp.int32),
            dma((4,)),
            pltpu.VMEM((2, 4, 4, 2, TOK_DEV, depth // 2), bf16),
            pltpu.VMEM((WIDE, depth), bf16),
            pltpu.VMEM((N_E, TOK_DEV, WIDE), bf16),
            pltpu.VMEM((8, TOK_DEV, WIDE), bf16),
            pltpu.VMEM((N_E, 1, WIDE), jnp.float32),
            pltpu.VMEM((N_T, GROUP, WIDE), bf16),
            pltpu.VMEM((N_T, GROUP, WIDE), bf16),
            pltpu.VMEM((GROUP, WIDE), jnp.float32),
            pltpu.VMEM((4, GROUP, WIDE), bf16),
            pltpu.VMEM((N_T, 4, GROUP, WIDE), bf16),
            pltpu.VMEM((N_E // 2, 2, TOK_DEV, FCOL), bf16),
            pltpu.VMEM((N_E // 2, TOK_DEV, FCOL), bf16),
            pltpu.VMEM((N_E // 2, TOK_DEV, FCOL), bf16),
            dma((4,)), dma((4,)),
            dma((16,)), dma((16,)), dma((8,)), dma((8,)),
            dma((N_E,)), dma((8,)), dma((N_T,)), dma((N_T,)), dma((4,)), dma((4,)), dma((4,)), dma((4,)),
            dma((3,)), dma((3,)), dma((N_E // 2,)), dma((N_E // 2,)), dma((2,)),
            pltpu.VMEM((8, TOK_DEV, GROUP), bf16), dma((8,)), dma((8,)),
            dma((40,)), dma((40,)), dma((128,)), dma((128,)),
            *[pltpu.VMEM((32, CAP, rows, columns), bf16) for _, _, _, rows in PARTS],
            *[
                pltpu.VMEM((blocks, rows, columns), bf16)
                for _, z_first, _, rows in PARTS
                for _ in range(7 if z_first else 3)
            ],
        ],
        compiler_params=pltpu.CompilerParams(
            collective_id=0, has_side_effects=True, vmem_limit_bytes=56 * 2**20
        ),
        name="step",
    )(
        master, grad, first, second, context, out_weight.T, hidden, norm_gain.reshape(1, -1), plan.reshape(8, 128)
    )


def finish_kernel(
    plan_in, route_in, partial_in, squares_in, roll, master_in, first_in, second_in,
    out, rollout, master, first, second,
    plan, route, stage, state, partial, square_parts, seen, in_sems, out_sems, state_in_sems, state_out_sems, decode_sems,
):
    e = lax.axis_index("expert")
    slots = rollout.shape[0]
    sources, targets = (master_in, first_in, second_in), (master, first, second)

    def fetch(j, place):
        return pltpu.make_async_copy(roll.at[place], stage.at[j], in_sems.at[j])

    def store(j):
        return pltpu.make_async_copy(stage.at[j], rollout.at[j], out_sems.at[j])

    def state_in(i):
        return pltpu.make_async_copy(sources[i], state.at[i], state_in_sems.at[i])

    def state_out(i):
        return pltpu.make_async_copy(state.at[i], targets[i], state_out_sems.at[i])

    partial_copy = pltpu.make_async_copy(partial_in, partial, decode_sems.at[0])
    squares_copy = pltpu.make_async_copy(squares_in, square_parts, decode_sems.at[1])
    plan_copy = pltpu.make_async_copy(plan_in, plan, decode_sems.at[2])
    route_copy = pltpu.make_async_copy(route_in, route, decode_sems.at[3])
    plan_copy.start()
    route_copy.start()
    for i in range(3):
        state_in(i).start()

    @pl.loop(0, N_E)
    def _(j):
        seen[j] = 0

    plan_copy.wait()
    route_copy.wait()

    @pl.loop(0, slots)
    def _(j):
        source = (plan[e * slots + j] * 9363) >> 16
        rank = seen[source]
        seen[source] = rank + 1
        dy = (source // 8 + 4 - e // 8) % 4
        dx = (source // 2 + 4 - (e // 2) % 4) % 4
        dz = (source + e) % 2
        fetch(j, ((dx * 4 + dy) * 2 + dz) * CAP + rank).start()

    partial_copy.start()
    squares_copy.start()
    for i in range(3):
        state_in(i).wait()
        state_out(i).start()

    @pl.loop(0, slots)
    def _(j):
        fetch(j, 0).wait()
        store(j).start()

    partial_copy.wait()
    squares_copy.wait()
    token = lax.broadcasted_iota(jnp.int32, (TOK_DEV, 1), 0)
    expert = jnp.zeros((TOK_DEV, 1), jnp.int32)
    for i in range(TOK_DEV):
        expert = jnp.where(token == i, route[e * TOK_DEV + i], expert)
    pre = jnp.zeros((TOK_DEV, FCOL), jnp.float32)
    squares = jnp.zeros((TOK_DEV, 1), jnp.float32)
    for k in range(4):
        total = jnp.zeros((TOK_DEV, FCOL), jnp.float32)
        for h in range(4):
            total = total + partial[k * 4 + h].astype(jnp.float32)
        pre = pre + jnp.where(expert == k, total, 0.0)
    for h in range(8):
        squares = squares + jnp.sum(square_parts[h].astype(jnp.float32), axis=1, keepdims=True)
    pre = pre * lax.rsqrt(squares / (N_E * COLS) + 1e-06)
    out[...] = (pre / (1.0 + jnp.exp(-pre))).astype(jnp.bfloat16)

    @pl.loop(0, slots)
    def _(j):
        store(j).wait()

    for i in range(3):
        state_out(i).wait()


def finish(plan, route, partial, squares, roll, state):
    vmem = pl.BlockSpec(memory_space=pltpu.VMEM)
    anywhere = pl.BlockSpec(memory_space=pl.ANY)
    block_rows, columns = roll.shape[-2:]
    slots = plan.shape[0] // N_E
    shape = jax.ShapeDtypeStruct(state[0].shape, jnp.float32)
    dma = pltpu.SemaphoreType.DMA
    return pl.pallas_call(
        finish_kernel,
        out_shape=(
            jax.ShapeDtypeStruct((TOK_DEV, FCOL), jnp.bfloat16),
            jax.ShapeDtypeStruct((slots, block_rows, columns), jnp.bfloat16),
            shape, shape, shape,
        ),
        in_specs=[anywhere] * 8,
        out_specs=(vmem,) + (anywhere,) * 4,
        scratch_shapes=[
            pltpu.SMEM(plan.shape, jnp.int32),
            pltpu.SMEM(route.shape, jnp.int32),
            pltpu.VMEM((slots, block_rows, columns), jnp.bfloat16),
            pltpu.VMEM((3, *state[0].shape), jnp.float32),
            pltpu.VMEM(partial.shape, partial.dtype),
            pltpu.VMEM(squares.shape, squares.dtype),
            pltpu.SMEM((N_E,), jnp.int32),
            dma((slots,)), dma((slots,)), dma((3,)), dma((3,)), dma((4,)),
        ],
        compiler_params=pltpu.CompilerParams(vmem_limit_bytes=56 * 2**20),
        name="finish",
    )(plan, route, partial, squares, roll.reshape(4 * 4 * 2 * CAP, block_rows, columns), *state)


def shards(
    master, grad, moment_one, moment_two, context, out_weight, hidden, norm_gain, route, plan
):
    partial, squares, roll, *state = step(
        master, grad, moment_one, moment_two, context, out_weight, hidden, norm_gain, plan
    )
    activation, rollout, *state = finish(plan, route, partial, squares, roll, state)
    return (*state, rollout, activation)


def solution(mesh):
    return jax.shard_map(
        shards,
        mesh=mesh,
        in_specs=(
            P("expert", None, "tensor"),
            P("expert", None, "tensor"),
            P("expert", None, "tensor"),
            P("expert", None, "tensor"),
            P("expert", "tensor"),
            P("tensor", "expert"),
            P("expert", None),
            P(),
            P(),
            P(),
        ),
        out_specs=(
            P("expert", None, "tensor"),
            P("expert", None, "tensor"),
            P("expert", None, "tensor"),
            P("expert", None, "tensor"),
            P("expert", "tensor"),
        ),
        check_vma=False,
    )
```
